512 devices in a mesh: req: 32 (over z, core), tensor: 16 (over y, x).
Axes of the slice: x: 4, y: 4, z: 16, core: 2. Of those that a mesh axis runs over, the one named last changes fastest.
Arguments:
- x_in: bfloat16 [36864, 8192], P(('req', 'tensor')), may hold values from -6 to 6
- dt_raw: bfloat16 [36864, 128], P(('req', 'tensor')), may hold values from -4 to 4
- b_in: bfloat16 [36864, 512], P(('req', 'tensor')), may hold values from -1 to 1
- c_in: bfloat16 [36864, 512], P(('req', 'tensor')), may hold values from -1 to 1
- a_log: float32 [128], P('tensor')
- dt_bias: float32 [128], P('tensor'), may hold values from -1 to 0
- d_skip: float32 [128], P('tensor'), may hold values from 0.5 to 1.5
- state_cache: bfloat16 [192, 128, 64, 128], P('req', 'tensor'), may hold values from -6 to 6
- group_sessions: int32 [32, 6], replicated, may hold values from 0 to 191, as said below
- owners: int32 [192], replicated, may hold values from 0 to 31, as said below
- cache_slots: int32 [192], replicated, may hold values from 0 to 5, as said below
- lengths: int32 [192], replicated, may hold values from 64 to 192, as said below
Outputs:
- y_out: bfloat16 [36864, 8192], P(('req', 'tensor'))
- new_cache: bfloat16 [192, 128, 64, 128], P('req', 'tensor')
The draws below stay inside these ranges and needn't reach their ends.
Inputs may be any that keep to these rules, and one draw needn't show every extreme that they name: `group_sessions`: every session number stands exactly once. `owners`: each owner holds exactly 6 sessions. No two sessions of one request group have the same owner. `cache_slots`: no two sessions share both owner and cache slot. `lengths`: some session has exactly 192 new tokens and some exactly 64.
All inputs are finite; a program needn't handle non-finite values.
Results may differ from the reference program's by a relative error of at most 0.0035.
Values may be sent and summed in bfloat16 or wider, within the bound.
No kernel may reach another device: no remote copies, remote signals or barrier semaphores. Data moves between devices by JAX's collectives and lax.ppermute only.
A program may use at most 64 MiB of HBM per device.

```python
import jax
import jax.numpy as jnp
from jax import lax

HEADS = 128
HEAD_DIM = 64
STATE = 128
GROUPS = 4
MAXLEN = 192
MINLEN = 64
SESS_GRP = 6
SESSIONS = 192
ROWS = 36864


def shuffle_row(sub_key):
    return jax.random.permutation(sub_key, SESS_GRP)


def routing_tables(key):
    groups_total = SESSIONS // SESS_GRP
    keys_all = jax.random.split(key, 6)
    owner_order = jax.random.permutation(keys_all[0], groups_total)
    base_shift = jax.random.randint(keys_all[1], (), 0, groups_total)
    offset_order = jax.random.permutation(keys_all[2], groups_total).astype(jnp.int32)
    spread_index = jnp.arange(SESS_GRP, dtype=jnp.int32) % groups_total
    shifts = offset_order[spread_index] + base_shift
    grid_index = (jnp.arange(groups_total, dtype=jnp.int32)[:, None] + shifts[None, :]) % groups_total
    owner_grid = owner_order[grid_index]
    slot_orders = jax.vmap(shuffle_row)(jax.random.split(keys_all[3], groups_total))
    column_index = jnp.broadcast_to(jnp.arange(SESS_GRP, dtype=jnp.int32)[None, :], owner_grid.shape)
    slot_grid = slot_orders[owner_grid, column_index]
    column_shuffle = jax.vmap(shuffle_row)(jax.random.split(keys_all[4], groups_total))
    owner_grid = jnp.take_along_axis(owner_grid, column_shuffle, axis=1)
    slot_grid = jnp.take_along_axis(slot_grid, column_shuffle, axis=1)
    session_grid = jax.random.permutation(keys_all[5], SESSIONS).reshape(groups_total, SESS_GRP).astype(jnp.int32)
    flat_sessions = session_grid.reshape(-1)
    owner_table = jnp.zeros((SESSIONS,), jnp.int32).at[flat_sessions].set(owner_grid.reshape(-1).astype(jnp.int32))
    slot_table = jnp.zeros((SESSIONS,), jnp.int32).at[flat_sessions].set(slot_grid.reshape(-1).astype(jnp.int32))
    return (session_grid, owner_table, slot_table)


def draw_group_sessions(key, part):
    tables = routing_tables(key)
    return tables[0]


def draw_owners(key, part):
    tables = routing_tables(key)
    return tables[1]


def draw_cache_slots(key, part):
    tables = routing_tables(key)
    return tables[2]


def draw_lengths(key, part):
    key = jax.random.fold_in(key, 11)
    keys_all = jax.random.split(key, 3)
    drawn = jax.random.randint(keys_all[0], (SESSIONS,), MINLEN, MAXLEN + 1)
    longest = jax.random.randint(keys_all[1], (), 0, SESSIONS)
    shortest = (longest + jax.random.randint(keys_all[2], (), 1, SESSIONS)) % SESSIONS
    drawn = drawn.at[longest].set(MAXLEN).at[shortest].set(MINLEN)
    return drawn.astype(jnp.int32)


def draw_a_log(key, part):
    key = jax.random.fold_in(key, 7)
    keys_all = jax.random.split(key, 3)
    fast_share = 5
    is_fast = jax.random.randint(keys_all[0], (HEADS,), 0, 10) < fast_share
    slow_log = jax.random.uniform(keys_all[1], (HEADS,), jnp.float32, jnp.log(0.2), jnp.log(2.0))
    fast_log = jax.random.uniform(keys_all[2], (HEADS,), jnp.float32, jnp.log(24.0), jnp.log(48.0))
    chosen = jnp.where(is_fast, fast_log, slow_log) - jnp.log(jnp.float32(MAXLEN))
    return chosen.astype(jnp.float32)


def block_scale(stream_key, dims, cuts, least, high):
    def one(dim, shards_of):
        steps = jax.random.uniform(jax.random.fold_in(jax.random.fold_in(stream_key, 6), dim), (shards_of,), jnp.float32, least / len(cuts), high / len(cuts))
        return jnp.repeat(jnp.exp(steps), dims[dim] // shards_of).reshape((-1,) + (1,) * (len(dims) - dim - 1))

    level = one(*cuts[0])
    for cut in cuts[1:]:
        level = level * one(*cut)
    return level


def centred(own_key, shape, scale, bound, cuts=(), held_as=jnp.bfloat16):
    result = scale * jax.random.normal(own_key, shape, jnp.float32)
    if cuts:
        result = result * block_scale(own_key, shape, cuts, -0.22, 0.18)
    return jnp.clip(result, -bound, bound).astype(held_as)


def setup_inputs(seed: int = 0) -> dict:
    key_of = jax.random.split(jax.random.key(seed), 13)
    return {
        "x_in": centred(key_of[0], (ROWS, HEADS * HEAD_DIM), 1.0, 6.0, ((0, 512),)),
        "dt_raw": centred(key_of[1], (ROWS, HEADS), 1.0, 4.0, ((0, 512),)),
        "b_in": centred(key_of[2], (ROWS, GROUPS * STATE), 0.07, 1.0, ((0, 512),)),
        "c_in": centred(key_of[3], (ROWS, GROUPS * STATE), 0.07, 1.0, ((0, 512),)),
        "a_log": draw_a_log(jax.random.fold_in(key_of[12], 71), 0),
        "dt_bias": jnp.clip(-1.0 + 1.0 * jax.random.uniform(key_of[5], (HEADS,), jnp.float32) ** block_scale(key_of[5], (HEADS,), ((0, 16),), -0.2, 0.2), -1.0, 0.0),
        "d_skip": jnp.clip(0.5 + 1.0 * jax.random.uniform(key_of[6], (HEADS,), jnp.float32) ** block_scale(key_of[6], (HEADS,), ((0, 16),), -0.2, 0.2), 0.5, 1.5),
        "state_cache": centred(key_of[7], (SESSIONS, HEADS, HEAD_DIM, STATE), 1.0, 6.0, ((0, 32), (1, 16))),
        "group_sessions": draw_group_sessions(jax.random.fold_in(key_of[12], 71), 0),
        "owners": draw_owners(jax.random.fold_in(key_of[12], 71), 0),
        "cache_slots": draw_cache_slots(jax.random.fold_in(key_of[12], 71), 0),
        "lengths": draw_lengths(jax.random.fold_in(key_of[12], 71), 0),
    }


def session_ssd(values, raw_steps, in_proj, out_proj, initial, length_now, decay_rate, step_bias, skip_gain):
    highest = lax.Precision.HIGHEST
    steps_total = values.shape[0]
    heads_total = values.shape[1]
    share = heads_total // in_proj.shape[1]
    places = jnp.arange(steps_total, dtype=jnp.int32)
    is_live = places < length_now
    step_size = jnp.where(is_live[:, None], jax.nn.softplus(raw_steps.astype(jnp.float32) + step_bias[None, :]), jnp.float32(0.0))
    cumulative = jnp.cumsum(step_size * decay_rate[None, :], axis=0)
    affinity = jnp.einsum('tgn,ugn->gtu', out_proj.astype(jnp.float32), in_proj.astype(jnp.float32), precision=highest)
    affinity = jnp.repeat(affinity, share, axis=0)
    causal = places[:, None] >= places[None, :]
    spread = cumulative.T[:, :, None] - cumulative.T[:, None, :]
    damping = jnp.exp(jnp.where(causal[None], spread, -jnp.inf))
    weights = (affinity * damping * step_size.T[:, None, :]).astype(jnp.bfloat16)
    local_mix = jnp.einsum('htu,uhp->thp', weights.astype(jnp.float32), values.astype(jnp.float32), precision=highest)
    readout = jnp.repeat(out_proj, share, axis=1).astype(jnp.float32)
    carried = jnp.einsum('hpn,thn->thp', initial, readout, precision=highest)
    mixed = local_mix + jnp.exp(cumulative)[:, :, None] * carried + skip_gain[None, :, None] * values.astype(jnp.float32)
    mixed = jnp.where(is_live[:, None, None], mixed, jnp.float32(0.0)).astype(jnp.bfloat16)
    to_end = jnp.exp(cumulative[-1][None, :] - cumulative) * step_size
    scaled = (values.astype(jnp.float32) * to_end[:, :, None]).astype(jnp.bfloat16)
    inputs_rep = jnp.repeat(in_proj, share, axis=1).astype(jnp.float32)
    closing = jnp.exp(cumulative[-1])[:, None, None] * initial + jnp.einsum('thp,thn->hpn', scaled.astype(jnp.float32), inputs_rep, precision=highest)
    return mixed, closing.astype(jnp.bfloat16)


def reference(x_in, dt_raw, b_in, c_in, a_log, dt_bias, d_skip, state_cache, group_sessions, owners, cache_slots, lengths):
    decay_rate = -jnp.exp(a_log)
    ordered = group_sessions.reshape(-1).astype(jnp.int32)
    cache_rows = (owners[ordered] * SESS_GRP + cache_slots[ordered]).astype(jnp.int32)
    session_lengths = lengths[ordered]
    value_blocks = x_in.reshape(SESSIONS, MAXLEN, HEADS, HEAD_DIM)
    step_blocks = dt_raw.reshape(SESSIONS, MAXLEN, HEADS)
    input_blocks = b_in.reshape(SESSIONS, MAXLEN, GROUPS, STATE)
    readout_blocks = c_in.reshape(SESSIONS, MAXLEN, GROUPS, STATE)

    def one_session(member):
        initial = state_cache[cache_rows[member]].astype(jnp.float32)
        return session_ssd(value_blocks[member], step_blocks[member], input_blocks[member], readout_blocks[member], initial, session_lengths[member], decay_rate, dt_bias, d_skip)

    mixed_all, closing_all = lax.map(one_session, jnp.arange(SESSIONS, dtype=jnp.int32))
    y_out = mixed_all.reshape(ROWS, HEADS * HEAD_DIM)
    new_cache = jnp.zeros_like(state_cache).at[cache_rows].set(closing_all)
    return y_out, new_cache
```

```python
import functools

import jax
import jax.numpy as jnp
from jax import lax
from jax.experimental import pallas as pl
from jax.experimental.pallas import tpu as pltpu
from jax.sharding import PartitionSpec as P

HEADS = 128
HEAD_DIM = 64
STATE = 128
GROUPS = 4
MAXLEN = 192
LANES = 128
VMEM_LIMIT = 48 * 1024 * 1024


def pack_kernel(x_ref, dt_ref, b_ref, c_ref, out_ref):
    width = x_ref.shape[1]
    out_ref[0, :, :width] = x_ref[...]
    out_ref[0, :, width : width + STATE] = b_ref[...]
    out_ref[0, :, width + STATE : width + 2 * STATE] = c_ref[...]
    out_ref[0, :, width + 2 * STATE :] = dt_ref[...]


def pack_tokens(x_in, dt_raw, b_in, c_in, parts):
    rows, columns = x_in.shape
    width = columns // parts
    share = parts // GROUPS
    total = width + 2 * STATE + HEADS
    return pl.pallas_call(
        pack_kernel,
        grid=(parts,),
        in_specs=[
            pl.BlockSpec((rows, width), lambda t: (0, t)),
            pl.BlockSpec((rows, HEADS), lambda t: (0, 0)),
            pl.BlockSpec((rows, STATE), lambda t: (0, t // share)),
            pl.BlockSpec((rows, STATE), lambda t: (0, t // share)),
        ],
        out_specs=pl.BlockSpec((1, rows, total), lambda t: (t, 0, 0)),
        out_shape=jax.ShapeDtypeStruct((parts, rows, total), x_in.dtype),
        compiler_params=pltpu.CompilerParams(vmem_limit_bytes=VMEM_LIMIT),
        name="pack_tokens",
    )(x_in, dt_raw, b_in, c_in)


def cache_row(sessions_ref, owners_ref, slots_ref, slot_count, index):
    session = sessions_ref[index]
    return owners_ref[session] * slot_count + slots_ref[session]


def order_kernel(sessions_ref, owners_ref, slots_ref, in_ref, out_ref, *, slot_count, to_owner):
    def step(index, carry):
        row = cache_row(sessions_ref, owners_ref, slots_ref, slot_count, index)
        if to_owner:
            out_ref[row] = in_ref[index]
        else:
            out_ref[index] = in_ref[row]
        return carry

    lax.fori_loop(0, in_ref.shape[0], step, 0, unroll=8)


def reorder(pieces, sessions, owners, slots, slot_count, to_owner):
    smem = pl.BlockSpec(memory_space=pltpu.SMEM)
    vmem = pl.BlockSpec(memory_space=pltpu.VMEM)
    return pl.pallas_call(
        functools.partial(order_kernel, slot_count=slot_count, to_owner=to_owner),
        in_specs=[smem, smem, smem, vmem],
        out_specs=vmem,
        out_shape=jax.ShapeDtypeStruct(pieces.shape, pieces.dtype),
        compiler_params=pltpu.CompilerParams(vmem_limit_bytes=VMEM_LIMIT),
        name="to_owner_order" if to_owner else "to_group_order",
    )(sessions, owners, slots, pieces)


def session_kernel(
    place_ref,
    sessions_ref,
    lengths_ref,
    packed_ref,
    start_ref,
    a_log_ref,
    bias_ref,
    skip_ref,
    y_ref,
    closing_ref,
    *,
    heads,
    slot_count,
):
    highest = lax.Precision.HIGHEST
    f32 = jnp.float32
    bf16 = jnp.bfloat16
    width = heads * HEAD_DIM
    rows = MAXLEN
    half = LANES
    session = sessions_ref[place_ref[0] * slot_count + pl.program_id(0)]
    length = lengths_ref[session]

    values = packed_ref[:, :width]
    in_proj = packed_ref[:, width : width + STATE]
    out_proj = packed_ref[:, width + STATE : width + 2 * STATE]
    all_steps = packed_ref[:, width + 2 * STATE :]

    lane_from = lax.broadcasted_iota(jnp.int32, (HEADS, LANES), 0)
    lane_to = lax.broadcasted_iota(jnp.int32, (HEADS, LANES), 1)
    chosen = ((lane_from == lane_to + place_ref[1] * heads) & (lane_to < heads)).astype(bf16)
    raw = jnp.dot(all_steps, chosen, preferred_element_type=f32)
    row_index = lax.broadcasted_iota(jnp.int32, (rows, LANES), 0)
    shifted = raw + bias_ref[...]
    soft = jnp.maximum(shifted, 0.0) + jnp.log(1.0 + jnp.exp(-jnp.abs(shifted)))
    step = jnp.where(row_index < length, soft, 0.0)
    rate = -jnp.exp(a_log_ref[...])
    t_index = lax.broadcasted_iota(jnp.int32, (rows, rows), 0)
    u_index = lax.broadcasted_iota(jnp.int32, (rows, rows), 1)
    causal = t_index >= u_index
    cum = jnp.dot(
        causal.astype(f32), step * rate, precision=highest, preferred_element_type=f32
    )
    drop = cum - jnp.log(step)
    last = cum[rows - 1 : rows, :]
    to_end = jnp.exp(last - cum) * step
    grown = jnp.exp(cum)
    drop_rows = drop.T

    affinity = lax.dot_general(
        out_proj, in_proj, (((1,), (1,)), ((), ())), preferred_element_type=f32
    )
    affinity = jnp.where(causal, affinity, 0.0)
    top, low = affinity[:half, :half], affinity[half:, :]

    start = start_ref[...].reshape(width, STATE)
    carried = lax.dot_general(
        out_proj, start, (((1,), (1,)), ((), ())), preferred_element_type=f32
    )
    live = row_index < length
    left = lax.broadcasted_iota(jnp.int32, (rows, LANES), 1) < HEAD_DIM

    def spread(columns, first):
        one = jnp.broadcast_to(columns[:, first : first + 1], (rows, LANES))
        two = jnp.broadcast_to(columns[:, first + 1 : first + 2], (rows, LANES))
        return jnp.where(left, one, two)

    scaled_parts = []
    for first in range(0, heads, 2):
        lanes = slice(first * HEAD_DIM, (first + 2) * HEAD_DIM)
        pair = values[:, lanes]
        mixed = []
        for head in (first, first + 1):
            column = cum[:, head : head + 1]
            line = drop_rows[head : head + 1, :]
            w_top = top * jnp.exp(jnp.minimum(column[:half] - line[:, :half], 80.0))
            w_low = low * jnp.exp(jnp.minimum(column[half:] - line, 80.0))
            mixed.append(
                jnp.concatenate(
                    [
                        jnp.dot(w_top.astype(bf16), pair[:half], preferred_element_type=f32),
                        jnp.dot(w_low.astype(bf16), pair, preferred_element_type=f32),
                    ],
                    axis=0,
                )
            )
        pair_f32 = pair.astype(f32)
        out = (
            jnp.where(left, mixed[0], mixed[1])
            + spread(grown, first) * carried[:, lanes]
            + skip_ref[:, lanes] * pair_f32
        )
        y_ref[:, lanes] = jnp.where(live, out, 0.0).astype(bf16)
        scaled_parts.append((pair_f32 * spread(to_end, first)).astype(bf16))
    scaled = jnp.concatenate(scaled_parts, axis=1)
    added = lax.dot_general(
        scaled, in_proj, (((0,), (0,)), ((), ())), preferred_element_type=f32
    )
    kept = jnp.exp(last)
    for head in range(heads):
        channels = slice(head * HEAD_DIM, (head + 1) * HEAD_DIM)
        closing = kept[:, head : head + 1] * start[channels].astype(f32) + added[channels]
        per = closing_ref.shape[2]
        begin = head * HEAD_DIM // per
        closing_ref[begin : begin + HEAD_DIM // per, 0] = closing.astype(bf16).reshape(
            HEAD_DIM // per, per, STATE
        )


def run_sessions(place, sessions, lengths, packed, start, a_log, dt_bias, d_skip):
    heads = a_log.shape[0]
    pieces, slot_count, per, _ = start.shape
    width = heads * HEAD_DIM
    pad = ((0, 0), (0, LANES - heads))
    a_row = jnp.pad(a_log[None, :], pad)
    bias_row = jnp.pad(dt_bias[None, :], pad)
    skip_row = jnp.repeat(d_skip, HEAD_DIM)[None, :]
    whole = lambda j, *_: (0, 0)
    return pl.pallas_call(
        functools.partial(session_kernel, heads=heads, slot_count=slot_count),
        grid_spec=pltpu.PrefetchScalarGridSpec(
            num_scalar_prefetch=3,
            grid=(slot_count,),
            in_specs=[
                pl.BlockSpec((MAXLEN, packed.shape[1]), lambda j, *_: (j, 0)),
                pl.BlockSpec((pieces, 1, per, STATE), lambda j, *_: (0, j, 0, 0)),
                pl.BlockSpec((1, LANES), whole),
                pl.BlockSpec((1, LANES), whole),
                pl.BlockSpec((1, width), whole),
            ],
            out_specs=[
                pl.BlockSpec((MAXLEN, width), lambda j, *_: (j, 0)),
                pl.BlockSpec((pieces, 1, per, STATE), lambda j, *_: (0, j, 0, 0)),
            ],
        ),
        out_shape=[
            jax.ShapeDtypeStruct((packed.shape[0], width), jnp.bfloat16),
            jax.ShapeDtypeStruct(start.shape, jnp.bfloat16),
        ],
        compiler_params=pltpu.CompilerParams(vmem_limit_bytes=VMEM_LIMIT),
        name="run_sessions",
    )(place, sessions, lengths, packed, start, a_row, bias_row, skip_row)


def per_device(
    x_in,
    dt_raw,
    b_in,
    c_in,
    a_log,
    dt_bias,
    d_skip,
    state_cache,
    group_sessions,
    owners,
    cache_slots,
    lengths,
):
    tensor_size = lax.axis_size("tensor")
    req_size = lax.axis_size("req")
    slot_count, heads = state_cache.shape[:2]
    per = heads * HEAD_DIM // req_size
    place = jnp.stack([lax.axis_index("req"), lax.axis_index("tensor")]).astype(jnp.int32)
    sessions = group_sessions.reshape(-1)

    pieces = state_cache.reshape(slot_count, req_size, per, STATE)
    spread = lax.all_to_all(pieces, "req", split_axis=1, concat_axis=0, tiled=False)
    spread = spread.reshape(req_size * slot_count, per, STATE)
    spread = reorder(spread, sessions, owners, cache_slots, slot_count, False)
    start = lax.all_to_all(
        spread.reshape(req_size, slot_count, per, STATE), "req", split_axis=0, concat_axis=0
    )

    packed = pack_tokens(x_in, dt_raw, b_in, c_in, tensor_size)
    packed = lax.all_to_all(packed, "tensor", split_axis=0, concat_axis=0)
    packed = packed.reshape(tensor_size * x_in.shape[0], packed.shape[2])

    mixed, closing = run_sessions(
        place, sessions, lengths, packed, start, a_log, dt_bias, d_skip
    )

    back = lax.all_to_all(closing, "req", split_axis=0, concat_axis=0)
    back = back.reshape(req_size * slot_count, per, STATE)
    back = reorder(back, sessions, owners, cache_slots, slot_count, True)
    back = lax.all_to_all(
        back.reshape(req_size, slot_count, per, STATE), "req", split_axis=0, concat_axis=0
    )
    new_cache = back.transpose(1, 0, 2, 3).reshape(state_cache.shape)

    shard = mixed.reshape(tensor_size, x_in.shape[0], heads * HEAD_DIM)
    y_out = lax.all_to_all(shard, "tensor", split_axis=0, concat_axis=0)
    y_out = y_out.transpose(1, 0, 2).reshape(x_in.shape)
    return y_out, new_cache


def solution(mesh):
    tokens = P(("req", "tensor"), None)
    states = P("req", "tensor", None, None)
    placed = (tokens,) * 4 + (P("tensor"),) * 3 + (states,) + (P(),) * 4
    return jax.shard_map(
        per_device,
        mesh=mesh,
        in_specs=placed,
        out_specs=(tokens, states),
        check_vma=False,
    )
```

```python
import functools

import jax
import jax.numpy as jnp
from jax import lax
from jax.experimental import pallas as pl
from jax.experimental.pallas import tpu as pltpu
from jax.sharding import PartitionSpec as P

HEADS = 128
HEAD_DIM = 64
STATE = 128
GROUPS = 4
MAXLEN = 192
LANES = 128
VMEM_LIMIT = 48 * 1024 * 1024


def pack_kernel(place_ref, x_ref, dt_ref, b_ref, c_ref, *out_refs):
    parts = len(out_refs)
    width = x_ref.shape[1] // parts
    share = parts // GROUPS
    for shift, out_ref in enumerate(out_refs):
        target = lax.rem(place_ref[1] + shift, parts)
        columns = pl.ds(pl.multiple_of(target * width, LANES), width)
        group = pl.ds(pl.multiple_of(target // share * STATE, LANES), STATE)
        out_ref[:, :width] = x_ref[:, columns]
        out_ref[:, width : width + STATE] = b_ref[:, group]
        out_ref[:, width + STATE : width + 2 * STATE] = c_ref[:, group]
        out_ref[:, width + 2 * STATE :] = dt_ref[...]


def gather_kernel(place_ref, *refs):
    out_ref = refs[-1]
    parts = len(refs) - 1
    for shift in range(parts):
        out_ref[lax.rem(place_ref[1] + parts - shift, parts)] = refs[shift][...]


def split_kernel(place_ref, rows_ref, *out_refs):
    parts = len(out_refs)
    for shift, out_ref in enumerate(out_refs):
        out_ref[...] = rows_ref[lax.rem(place_ref[1] + shift, parts)]


def columns_kernel(place_ref, *refs):
    out_ref = refs[-1]
    parts = len(refs) - 1
    width = refs[0].shape[1]
    for shift in range(parts):
        source = lax.rem(place_ref[1] + parts - shift, parts)
        out_ref[:, pl.ds(pl.multiple_of(source * width, LANES), width)] = refs[shift][...]


def local_call(kernel, place, arrays, out_shape, name):
    smem = pl.BlockSpec(memory_space=pltpu.SMEM)
    vmem = pl.BlockSpec(memory_space=pltpu.VMEM)
    several = isinstance(out_shape, list)
    return pl.pallas_call(
        kernel,
        in_specs=[smem] + [vmem] * len(arrays),
        out_specs=[vmem] * len(out_shape) if several else vmem,
        out_shape=out_shape,
        compiler_params=pltpu.CompilerParams(vmem_limit_bytes=VMEM_LIMIT),
        name=name,
    )(place, *arrays)


def send_shifted(arrays, axis):
    parts = len(arrays)
    moved = [arrays[0]]
    for shift in range(1, parts):
        moved.append(
            lax.ppermute(arrays[shift], axis, [(i, (i + shift) % parts) for i in range(parts)])
        )
    return moved


def cache_row(sessions_ref, owners_ref, slots_ref, slot_count, index):
    session = sessions_ref[index]
    return owners_ref[session] * slot_count + slots_ref[session]


def order_kernel(sessions_ref, owners_ref, slots_ref, in_ref, out_ref, *, slot_count, to_owner):
    def step(index, carry):
        row = cache_row(sessions_ref, owners_ref, slots_ref, slot_count, index)
        if to_owner:
            out_ref[row] = in_ref[index]
        else:
            out_ref[index] = in_ref[row]
        return carry

    lax.fori_loop(0, in_ref.shape[0], step, 0, unroll=8)


def reorder(pieces, sessions, owners, slots, slot_count, to_owner):
    smem = pl.BlockSpec(memory_space=pltpu.SMEM)
    vmem = pl.BlockSpec(memory_space=pltpu.VMEM)
    return pl.pallas_call(
        functools.partial(order_kernel, slot_count=slot_count, to_owner=to_owner),
        in_specs=[smem, smem, smem, vmem],
        out_specs=vmem,
        out_shape=jax.ShapeDtypeStruct(pieces.shape, pieces.dtype),
        compiler_params=pltpu.CompilerParams(vmem_limit_bytes=VMEM_LIMIT),
        name="to_owner_order" if to_owner else "to_group_order",
    )(sessions, owners, slots, pieces)


def session_kernel(
    place_ref,
    sessions_ref,
    lengths_ref,
    packed_ref,
    start_ref,
    a_log_ref,
    bias_ref,
    skip_ref,
    y_ref,
    closing_ref,
    *,
    heads,
    slot_count,
):
    highest = lax.Precision.HIGHEST
    f32 = jnp.float32
    bf16 = jnp.bfloat16
    width = heads * HEAD_DIM
    rows = MAXLEN
    half = LANES
    session = sessions_ref[place_ref[0] * slot_count + pl.program_id(0)]
    length = lengths_ref[session]

    values = packed_ref[:, :width]
    in_proj = packed_ref[:, width : width + STATE]
    out_proj = packed_ref[:, width + STATE : width + 2 * STATE]
    all_steps = packed_ref[:, width + 2 * STATE :]

    lane_from = lax.broadcasted_iota(jnp.int32, (HEADS, LANES), 0)
    lane_to = lax.broadcasted_iota(jnp.int32, (HEADS, LANES), 1)
    chosen = ((lane_from == lane_to + place_ref[1] * heads) & (lane_to < heads)).astype(bf16)
    raw = jnp.dot(all_steps, chosen, preferred_element_type=f32)
    row_index = lax.broadcasted_iota(jnp.int32, (rows, LANES), 0)
    shifted = raw + bias_ref[...]
    soft = jnp.maximum(shifted, 0.0) + jnp.log(1.0 + jnp.exp(-jnp.abs(shifted)))
    step = jnp.where(row_index < length, soft, 0.0)
    rate = -jnp.exp(a_log_ref[...])
    t_index = lax.broadcasted_iota(jnp.int32, (rows, rows), 0)
    u_index = lax.broadcasted_iota(jnp.int32, (rows, rows), 1)
    causal = t_index >= u_index
    cum = jnp.dot(
        causal.astype(f32), step * rate, precision=highest, preferred_element_type=f32
    )
    drop = cum - jnp.log(step)
    last = cum[rows - 1 : rows, :]
    to_end = jnp.exp(last - cum) * step
    grown = jnp.exp(cum)
    drop_rows = drop.T

    affinity = lax.dot_general(
        out_proj, in_proj, (((1,), (1,)), ((), ())), preferred_element_type=f32
    )
    affinity = jnp.where(causal, affinity, 0.0)
    top, low = affinity[:half, :half], affinity[half:, :]

    start = start_ref[...].reshape(width, STATE)
    carried = lax.dot_general(
        out_proj, start, (((1,), (1,)), ((), ())), preferred_element_type=f32
    )
    live = row_index < length
    left = lax.broadcasted_iota(jnp.int32, (rows, LANES), 1) < HEAD_DIM

    def spread(columns, first):
        one = jnp.broadcast_to(columns[:, first : first + 1], (rows, LANES))
        two = jnp.broadcast_to(columns[:, first + 1 : first + 2], (rows, LANES))
        return jnp.where(left, one, two)

    scaled_parts = []
    for first in range(0, heads, 2):
        lanes = slice(first * HEAD_DIM, (first + 2) * HEAD_DIM)
        pair = values[:, lanes]
        mixed = []
        for head in (first, first + 1):
            column = cum[:, head : head + 1]
            line = drop_rows[head : head + 1, :]
            w_top = top * jnp.exp(jnp.minimum(column[:half] - line[:, :half], 80.0))
            w_low = low * jnp.exp(jnp.minimum(column[half:] - line, 80.0))
            mixed.append(
                jnp.concatenate(
                    [
                        jnp.dot(w_top.astype(bf16), pair[:half], preferred_element_type=f32),
                        jnp.dot(w_low.astype(bf16), pair, preferred_element_type=f32),
                    ],
                    axis=0,
                )
            )
        pair_f32 = pair.astype(f32)
        out = (
            jnp.where(left, mixed[0], mixed[1])
            + spread(grown, first) * carried[:, lanes]
            + skip_ref[:, lanes] * pair_f32
        )
        y_ref[:, lanes] = jnp.where(live, out, 0.0).astype(bf16)
        scaled_parts.append((pair_f32 * spread(to_end, first)).astype(bf16))
    scaled = jnp.concatenate(scaled_parts, axis=1)
    added = lax.dot_general(
        scaled, in_proj, (((0,), (0,)), ((), ())), preferred_element_type=f32
    )
    kept = jnp.exp(last)
    for head in range(heads):
        channels = slice(head * HEAD_DIM, (head + 1) * HEAD_DIM)
        closing = kept[:, head : head + 1] * start[channels].astype(f32) + added[channels]
        per = closing_ref.shape[2]
        begin = head * HEAD_DIM // per
        closing_ref[begin : begin + HEAD_DIM // per, 0] = closing.astype(bf16).reshape(
            HEAD_DIM // per, per, STATE
        )


def run_sessions(place, sessions, lengths, packed, start, a_log, dt_bias, d_skip):
    heads = a_log.shape[0]
    pieces, slot_count, per, _ = start.shape
    width = heads * HEAD_DIM
    pad = ((0, 0), (0, LANES - heads))
    a_row = jnp.pad(a_log[None, :], pad)
    bias_row = jnp.pad(dt_bias[None, :], pad)
    skip_row = jnp.repeat(d_skip, HEAD_DIM)[None, :]
    whole = lambda j, *_: (0, 0)
    return pl.pallas_call(
        functools.partial(session_kernel, heads=heads, slot_count=slot_count),
        grid_spec=pltpu.PrefetchScalarGridSpec(
            num_scalar_prefetch=3,
            grid=(slot_count,),
            in_specs=[
                pl.BlockSpec((MAXLEN, packed.shape[1]), lambda j, *_: (j, 0)),
                pl.BlockSpec((pieces, 1, per, STATE), lambda j, *_: (0, j, 0, 0)),
                pl.BlockSpec((1, LANES), whole),
                pl.BlockSpec((1, LANES), whole),
                pl.BlockSpec((1, width), whole),
            ],
            out_specs=[
                pl.BlockSpec((MAXLEN, width), lambda j, *_: (j, 0)),
                pl.BlockSpec((pieces, 1, per, STATE), lambda j, *_: (0, j, 0, 0)),
            ],
        ),
        out_shape=[
            jax.ShapeDtypeStruct((packed.shape[0], width), jnp.bfloat16),
            jax.ShapeDtypeStruct(start.shape, jnp.bfloat16),
        ],
        compiler_params=pltpu.CompilerParams(vmem_limit_bytes=VMEM_LIMIT),
        name="run_sessions",
    )(place, sessions, lengths, packed, start, a_row, bias_row, skip_row)


def per_device(
    x_in,
    dt_raw,
    b_in,
    c_in,
    a_log,
    dt_bias,
    d_skip,
    state_cache,
    group_sessions,
    owners,
    cache_slots,
    lengths,
):
    tensor_size = lax.axis_size("tensor")
    req_size = lax.axis_size("req")
    slot_count, heads = state_cache.shape[:2]
    per = heads * HEAD_DIM // req_size
    place = jnp.stack([lax.axis_index("req"), lax.axis_index("tensor")]).astype(jnp.int32)
    sessions = group_sessions.reshape(-1)

    pieces = state_cache.reshape(slot_count, req_size, per, STATE)
    spread = lax.all_to_all(pieces, "req", split_axis=1, concat_axis=0, tiled=False)
    spread = spread.reshape(req_size * slot_count, per, STATE)
    spread = reorder(spread, sessions, owners, cache_slots, slot_count, False)
    start = lax.all_to_all(
        spread.reshape(req_size, slot_count, per, STATE), "req", split_axis=0, concat_axis=0
    )

    rows = x_in.shape[0]
    width = heads * HEAD_DIM
    total = width + 2 * STATE + HEADS
    piece = jax.ShapeDtypeStruct((rows, total), jnp.bfloat16)
    sent = local_call(
        pack_kernel, place, (x_in, dt_raw, b_in, c_in), [piece] * tensor_size, "pack_tokens"
    )
    packed = local_call(
        gather_kernel,
        place,
        send_shifted(sent, "tensor"),
        jax.ShapeDtypeStruct((tensor_size, rows, total), jnp.bfloat16),
        "gather_tokens",
    ).reshape(tensor_size * rows, total)

    mixed, closing = run_sessions(
        place, sessions, lengths, packed, start, a_log, dt_bias, d_skip
    )

    back = lax.all_to_all(closing, "req", split_axis=0, concat_axis=0)
    back = back.reshape(req_size * slot_count, per, STATE)
    back = reorder(back, sessions, owners, cache_slots, slot_count, True)
    back = lax.all_to_all(
        back.reshape(req_size, slot_count, per, STATE), "req", split_axis=0, concat_axis=0
    )
    new_cache = back.transpose(1, 0, 2, 3).reshape(state_cache.shape)

    sent = local_call(
        split_kernel,
        place,
        (mixed.reshape(tensor_size, rows, width),),
        [jax.ShapeDtypeStruct((rows, width), jnp.bfloat16)] * tensor_size,
        "split_rows",
    )
    y_out = local_call(
        columns_kernel,
        place,
        send_shifted(sent, "tensor"),
        jax.ShapeDtypeStruct(x_in.shape, jnp.bfloat16),
        "join_columns",
    )
    return y_out, new_cache


def solution(mesh):
    tokens = P(("req", "tensor"), None)
    states = P("req", "tensor", None, None)
    placed = (tokens,) * 4 + (P("tensor"),) * 3 + (states,) + (P(),) * 4
    return jax.shard_map(
        per_device,
        mesh=mesh,
        in_specs=placed,
        out_specs=(tokens, states),
        check_vma=False,
    )
```

```python
import functools

import jax
import jax.numpy as jnp
from jax import lax
from jax.experimental import pallas as pl
from jax.experimental.pallas import tpu as pltpu
from jax.sharding import PartitionSpec as P

HEADS = 128
HEAD_DIM = 64
STATE = 128
GROUPS = 4
MAXLEN = 192
LANES = 128
VMEM_LIMIT = 48 * 1024 * 1024


def pack_kernel(place_ref, x_ref, dt_ref, b_ref, c_ref, proj_ref, *out_refs):
    parts = len(out_refs)
    width = x_ref.shape[1] // parts
    group = place_ref[2]
    for shift, out_ref in enumerate(out_refs):
        target = lax.rem(group + shift, parts)
        out_ref[...] = x_ref[:, pl.ds(pl.multiple_of(target * width, LANES), width)]
    wide = b_ref.shape[1]
    proj_ref[:, :wide] = b_ref[...]
    proj_ref[:, wide : 2 * wide] = c_ref[...]
    proj_ref[:, 2 * wide :] = dt_ref[...]


def turn_in_kernel(place_ref, *refs):
    half = len(refs) // 2
    width = refs[0].shape[1] // half
    for shift in range(half):
        target = lax.rem(place_ref[3] + shift, half)
        columns = pl.ds(pl.multiple_of(target * width, LANES), width)
        for row in range(half):
            refs[half + shift][row] = refs[row][:, columns]


def gather_kernel(place_ref, *refs):
    out_ref = refs[-1]
    parts = len(refs) - 1
    for across in range(parts):
        x_from = lax.rem(place_ref[3] + parts - across, parts)
        for down in range(parts):
            y_from = lax.rem(place_ref[2] + parts - down, parts)
            out_ref[y_from * parts + x_from] = refs[across][down]


def split_kernel(place_ref, rows_ref, *out_refs):
    parts = len(out_refs)
    for across, out_ref in enumerate(out_refs):
        x_to = lax.rem(place_ref[3] + across, parts)
        for down in range(parts):
            y_to = lax.rem(place_ref[2] + down, parts)
            out_ref[down] = rows_ref[y_to * parts + x_to]


def turn_out_kernel(place_ref, *refs):
    half = len(refs) // 2
    width = refs[0].shape[2]
    for across in range(half):
        x_from = lax.rem(place_ref[3] + half - across, half)
        columns = pl.ds(pl.multiple_of(x_from * width, LANES), width)
        for down in range(half):
            refs[half + down][:, columns] = refs[across][down]


def columns_kernel(place_ref, *refs):
    out_ref = refs[-1]
    parts = len(refs) - 1
    width = refs[0].shape[1]
    for shift in range(parts):
        source = lax.rem(place_ref[2] + parts - shift, parts)
        out_ref[:, pl.ds(pl.multiple_of(source * width, LANES), width)] = refs[shift][...]


def local_call(kernel, place, arrays, out_shape, name):
    smem = pl.BlockSpec(memory_space=pltpu.SMEM)
    vmem = pl.BlockSpec(memory_space=pltpu.VMEM)
    several = isinstance(out_shape, list)
    return pl.pallas_call(
        kernel,
        in_specs=[smem] + [vmem] * len(arrays),
        out_specs=[vmem] * len(out_shape) if several else vmem,
        out_shape=out_shape,
        compiler_params=pltpu.CompilerParams(vmem_limit_bytes=VMEM_LIMIT),
        name=name,
    )(place, *arrays)


def send_along(arrays, count, along_y):
    moved = [arrays[0]]
    for shift in range(1, count):
        if along_y:
            pairs = [
                (i, (i // count + shift) % count * count + i % count) for i in range(count * count)
            ]
        else:
            pairs = [
                (i, i // count * count + (i % count + shift) % count) for i in range(count * count)
            ]
        moved.append(lax.ppermute(arrays[shift], "tensor", pairs))
    return moved


def cache_row(sessions_ref, owners_ref, slots_ref, slot_count, index):
    session = sessions_ref[index]
    return owners_ref[session] * slot_count + slots_ref[session]


def outgoing_kernel(sessions_ref, owners_ref, slots_ref, state_ref, delta_ref, out_ref):
    slot_count = delta_ref.shape[1]

    def step(group, carry):
        for slot in range(slot_count):
            row = cache_row(
                sessions_ref, owners_ref, slots_ref, slot_count, group * slot_count + slot
            )
            out_ref[group, slot] = state_ref[row]
            out_ref[group, slot_count + slot] = delta_ref[group, slot]
        return carry

    lax.fori_loop(0, delta_ref.shape[0], step, 0)


def closing_kernel(
    place_ref, sessions_ref, owners_ref, slots_ref, kept_ref, state_ref, arrived_ref, out_ref, *, heads
):
    groups, slots_twice, per, _ = arrived_ref.shape
    slot_count = slots_twice // 2
    head = place_ref[0] * per // HEAD_DIM

    def step(group, carry):
        for slot in range(slot_count):
            index = group * slot_count + slot
            row = cache_row(sessions_ref, owners_ref, slots_ref, slot_count, index)
            kept = kept_ref[index * heads + head]
            added = arrived_ref[group, slot_count + slot].astype(jnp.float32)
            closing = kept * state_ref[row].astype(jnp.float32) + added
            out_ref[row] = closing.astype(out_ref.dtype)
        return carry

    lax.fori_loop(0, groups, step, 0)


def token_steps(place_ref, steps_ref, bias_ref, a_log_ref, length, heads):
    f32 = jnp.float32
    lane_from = lax.broadcasted_iota(jnp.int32, (HEADS, LANES), 0)
    lane_to = lax.broadcasted_iota(jnp.int32, (HEADS, LANES), 1)
    chosen = (lane_from == lane_to + place_ref[1] * heads) & (lane_to < heads)
    raw = jnp.dot(steps_ref[...], chosen.astype(jnp.bfloat16), preferred_element_type=f32)
    row_index = lax.broadcasted_iota(jnp.int32, (MAXLEN, LANES), 0)
    shifted = raw + bias_ref[...]
    soft = jnp.maximum(shifted, 0.0) + jnp.log(1.0 + jnp.exp(-jnp.abs(shifted)))
    live = row_index < length
    step = jnp.where(live, soft, 0.0)
    t_index = lax.broadcasted_iota(jnp.int32, (MAXLEN, MAXLEN), 0)
    u_index = lax.broadcasted_iota(jnp.int32, (MAXLEN, MAXLEN), 1)
    causal = t_index >= u_index
    cum = jnp.dot(
        causal.astype(f32),
        step * -jnp.exp(a_log_ref[...]),
        precision=lax.Precision.HIGHEST,
        preferred_element_type=f32,
    )
    return step, cum, live, causal


def spread(columns, first, left):
    one = jnp.broadcast_to(columns[:, first : first + 1], left.shape)
    two = jnp.broadcast_to(columns[:, first + 1 : first + 2], left.shape)
    return jnp.where(left, one, two)


def left_half():
    return lax.broadcasted_iota(jnp.int32, (MAXLEN, LANES), 1) < HEAD_DIM


def delta_kernel(
    place_ref, sessions_ref, lengths_ref, x_ref, b_ref, steps_ref, a_log_ref, bias_ref,
    delta_ref, kept_ref, *, heads, slot_count
):
    length = lengths_ref[sessions_ref[place_ref[0] * slot_count + pl.program_id(0)]]
    step, cum, _, _ = token_steps(place_ref, steps_ref, bias_ref, a_log_ref, length, heads)
    last = cum[MAXLEN - 1 : MAXLEN, :]
    to_end = jnp.exp(last - cum) * step
    kept_ref[0] = jnp.broadcast_to(jnp.exp(last), kept_ref.shape[1:])
    left = left_half()
    in_proj = b_ref[...]
    per = delta_ref.shape[2]
    for first in range(0, heads, 2):
        lanes = slice(first * HEAD_DIM, (first + 2) * HEAD_DIM)
        scaled = x_ref[:, lanes].astype(jnp.float32) * spread(to_end, first, left)
        added = lax.dot_general(
            scaled.astype(jnp.bfloat16),
            in_proj,
            (((0,), (0,)), ((), ())),
            preferred_element_type=jnp.float32,
        )
        begin, count = first * HEAD_DIM // per, 2 * HEAD_DIM // per
        delta_ref[begin : begin + count, 0] = added.astype(jnp.bfloat16).reshape(
            count, per, STATE
        )


def local_kernel(
    place_ref, sessions_ref, lengths_ref, x_ref, b_ref, c_ref, steps_ref, a_log_ref, bias_ref,
    skip_ref, local_ref, grown_ref, *, heads, slot_count
):
    f32 = jnp.float32
    bf16 = jnp.bfloat16
    half = LANES
    length = lengths_ref[sessions_ref[place_ref[0] * slot_count + pl.program_id(0)]]
    step, cum, live, causal = token_steps(
        place_ref, steps_ref, bias_ref, a_log_ref, length, heads
    )
    drop_rows = (cum - jnp.log(step)).T
    grown_ref[...] = jnp.where(live, jnp.exp(cum), 0.0)
    affinity = lax.dot_general(
        c_ref[...], b_ref[...], (((1,), (1,)), ((), ())), preferred_element_type=f32
    )
    affinity = jnp.where(causal, affinity, 0.0)
    top, low = affinity[:half, :half], affinity[half:, :]
    left = left_half()
    for first in range(0, heads, 2):
        lanes = slice(first * HEAD_DIM, (first + 2) * HEAD_DIM)
        pair = x_ref[:, lanes]
        mixed = []
        for head in (first, first + 1):
            column = cum[:, head : head + 1]
            line = drop_rows[head : head + 1, :]
            w_top = top * jnp.exp(jnp.minimum(column[:half] - line[:, :half], 80.0))
            w_low = low * jnp.exp(jnp.minimum(column[half:] - line, 80.0))
            mixed.append(
                jnp.concatenate(
                    [
                        jnp.dot(w_top.astype(bf16), pair[:half], preferred_element_type=f32),
                        jnp.dot(w_low.astype(bf16), pair, preferred_element_type=f32),
                    ],
                    axis=0,
                )
            )
        out = jnp.where(left, mixed[0], mixed[1]) + skip_ref[:, lanes] * pair.astype(f32)
        local_ref[:, lanes] = jnp.where(live, out, 0.0)


def carry_kernel(place_ref, c_ref, start_ref, local_ref, grown_ref, y_ref, *, heads):
    width = heads * HEAD_DIM
    start = start_ref[...].reshape(width, STATE)
    carried = lax.dot_general(
        c_ref[...], start, (((1,), (1,)), ((), ())), preferred_element_type=jnp.float32
    )
    grown = grown_ref[...]
    left = left_half()
    for first in range(0, heads, 2):
        lanes = slice(first * HEAD_DIM, (first + 2) * HEAD_DIM)
        out = local_ref[:, lanes] + spread(grown, first, left) * carried[:, lanes]
        y_ref[:, lanes] = out.astype(jnp.bfloat16)


def session_call(kernel, scalars, slot_count, operands, outputs, flops, name):
    return pl.pallas_call(
        kernel,
        grid_spec=pltpu.PrefetchScalarGridSpec(
            num_scalar_prefetch=len(scalars),
            grid=(slot_count,),
            in_specs=[pl.BlockSpec(block, index) for _, block, index in operands],
            out_specs=[pl.BlockSpec(block, index) for _, block, index in outputs],
        ),
        out_shape=[shape for shape, _, _ in outputs],
        compiler_params=pltpu.CompilerParams(vmem_limit_bytes=VMEM_LIMIT),
        cost_estimate=pl.CostEstimate(
            flops=flops, bytes_accessed=8 * 1024 * 1024, transcendentals=0
        ),
        name=name,
    )(*scalars, *(array for array, _, _ in operands))


def per_device(
    x_in,
    dt_raw,
    b_in,
    c_in,
    a_log,
    dt_bias,
    d_skip,
    state_cache,
    group_sessions,
    owners,
    cache_slots,
    lengths,
):
    tensor_size = lax.axis_size("tensor")
    req_size = lax.axis_size("req")
    slot_count, heads = state_cache.shape[:2]
    per = heads * HEAD_DIM // req_size
    side = tensor_size // GROUPS
    rows = x_in.shape[0]
    width = heads * HEAD_DIM
    bf16 = jnp.bfloat16
    f32 = jnp.float32
    shape = jax.ShapeDtypeStruct
    req_index = lax.axis_index("req")
    tensor_index = lax.axis_index("tensor")
    place = jnp.stack(
        [req_index, tensor_index, tensor_index // side, tensor_index % side]
    ).astype(jnp.int32)
    sessions = group_sessions.reshape(-1)
    smem = pl.BlockSpec(memory_space=pltpu.SMEM)
    vmem = pl.BlockSpec(memory_space=pltpu.VMEM)
    params = pltpu.CompilerParams(vmem_limit_bytes=VMEM_LIMIT)

    pieces = state_cache.reshape(slot_count, req_size, per, STATE)
    held = lax.all_to_all(pieces, "req", split_axis=1, concat_axis=0, tiled=False)
    held = held.reshape(req_size * slot_count, per, STATE)

    proj, *sent = local_call(
        pack_kernel,
        place,
        (x_in, dt_raw, b_in, c_in),
        [shape((rows, 2 * GROUPS * STATE + HEADS), bf16)]
        + [shape((rows, side * width), bf16)] * GROUPS,
        "pack_tokens",
    )
    proj = lax.all_gather(proj, "tensor", axis=0, tiled=True)
    sent = local_call(
        turn_in_kernel,
        place,
        send_along(sent, side, True),
        [shape((GROUPS, rows, width), bf16)] * side,
        "turn_in",
    )
    tokens = local_call(
        gather_kernel,
        place,
        send_along(sent, side, False),
        shape((tensor_size, rows, width), bf16),
        "gather_tokens",
    ).reshape(tensor_size * rows, width)

    pad = ((0, 0), (0, LANES - heads))
    a_row = jnp.pad(a_log[None, :], pad)
    bias_row = jnp.pad(dt_bias[None, :], pad)
    skip_row = jnp.repeat(d_skip, HEAD_DIM)[None, :]
    one_row = lambda j, *_: (0, 0)
    by_session = lambda j, *_: (j, 0)
    x_op = (tokens, (MAXLEN, width), by_session)
    b_op = (proj, (MAXLEN, STATE), lambda j, place, *_: (j, place[2]))
    c_op = (proj, (MAXLEN, STATE), lambda j, place, *_: (j, GROUPS + place[2]))
    steps_op = (proj, (MAXLEN, HEADS), lambda j, *_: (j, 2 * GROUPS))
    a_op = (a_row, (1, LANES), one_row)
    bias_op = (bias_row, (1, LANES), one_row)
    skip_op = (skip_row, (1, width), one_row)
    scalars = (place, sessions, lengths)
    sizes = dict(heads=heads, slot_count=slot_count)
    piece_block = (req_size, 1, per, STATE)
    by_slot = lambda j, *_: (0, j, 0, 0)
    total_rows = tensor_size * rows

    delta, kept = session_call(
        functools.partial(delta_kernel, **sizes),
        scalars,
        slot_count,
        [x_op, b_op, steps_op, a_op, bias_op],
        [
            (shape((req_size, slot_count, per, STATE), bf16), piece_block, by_slot),
            (shape((slot_count, 8, LANES), f32), (1, 8, LANES), lambda j, *_: (j, 0, 0)),
        ],
        4_000_000_000,
        "delta_states",
    )
    kept = lax.all_gather(kept[:, 0, :heads], "req", axis=0, tiled=True).reshape(-1)

    outgoing = pl.pallas_call(
        outgoing_kernel,
        in_specs=[smem, smem, smem, vmem, vmem],
        out_specs=vmem,
        out_shape=shape((req_size, 2 * slot_count, per, STATE), bf16),
        compiler_params=params,
        name="starts_and_deltas",
    )(sessions, owners, cache_slots, held, delta)
    arrived = lax.all_to_all(outgoing, "req", split_axis=0, concat_axis=0)

    local, grown = session_call(
        functools.partial(local_kernel, **sizes),
        scalars,
        slot_count,
        [x_op, b_op, c_op, steps_op, a_op, bias_op, skip_op],
        [
            (shape((total_rows, width), f32), (MAXLEN, width), by_session),
            (shape((total_rows, LANES), f32), (MAXLEN, LANES), by_session),
        ],
        10_000_000_000,
        "local_part",
    )

    closing = pl.pallas_call(
        functools.partial(closing_kernel, heads=heads),
        in_specs=[smem] * 5 + [vmem] * 2,
        out_specs=vmem,
        out_shape=shape(held.shape, bf16),
        compiler_params=params,
        name="closing_states",
    )(place, sessions, owners, cache_slots, kept, held, arrived)
    closing, arrived = lax.optimization_barrier((closing, arrived))
    back = lax.all_to_all(
        closing.reshape(req_size, slot_count, per, STATE), "req", split_axis=0, concat_axis=0
    )
    new_cache = back.transpose(1, 0, 2, 3).reshape(state_cache.shape)

    (mixed,) = session_call(
        functools.partial(carry_kernel, heads=heads),
        (place,),
        slot_count,
        [
            c_op,
            (arrived, piece_block, by_slot),
            (local, (MAXLEN, width), by_session),
            (grown, (MAXLEN, LANES), by_session),
        ],
        [(shape((total_rows, width), bf16), (MAXLEN, width), by_session)],
        3_000_000_000,
        "carried_part",
    )
    sent = local_call(
        split_kernel,
        place,
        (mixed.reshape(tensor_size, rows, width),),
        [shape((GROUPS, rows, width), bf16)] * side,
        "split_rows",
    )
    sent = local_call(
        turn_out_kernel,
        place,
        send_along(sent, side, False),
        [shape((rows, side * width), bf16)] * GROUPS,
        "turn_out",
    )
    y_out = local_call(
        columns_kernel,
        place,
        send_along(sent, side, True),
        shape(x_in.shape, bf16),
        "join_columns",
    )
    return y_out, new_cache


def solution(mesh):
    tokens = P(("req", "tensor"), None)
    states = P("req", "tensor", None, None)
    placed = (tokens,) * 4 + (P("tensor"),) * 3 + (states,) + (P(),) * 4
    return jax.shard_map(
        per_device,
        mesh=mesh,
        in_specs=placed,
        out_specs=(tokens, states),
        check_vma=False,
    )
```

```python
import functools

import jax
import jax.numpy as jnp
from jax import lax
from jax.experimental import pallas as pl
from jax.experimental.pallas import tpu as pltpu
from jax.sharding import PartitionSpec as P

HEADS = 128
HEAD_DIM = 64
STATE = 128
GROUPS = 4
MAXLEN = 192
LANES = 128
VMEM_LIMIT = 48 * 1024 * 1024


def pack_kernel(place_ref, x_ref, dt_ref, b_ref, c_ref, proj_ref, *out_refs):
    parts = len(out_refs)
    width = x_ref.shape[1] // parts
    group = place_ref[2]
    for shift, out_ref in enumerate(out_refs):
        target = lax.rem(group + shift, parts)
        out_ref[...] = x_ref[:, pl.ds(pl.multiple_of(target * width, LANES), width)]
    wide = b_ref.shape[1]
    proj_ref[:, :wide] = b_ref[...]
    proj_ref[:, wide : 2 * wide] = c_ref[...]
    proj_ref[:, 2 * wide :] = dt_ref[...]


def turn_in_kernel(place_ref, *refs):
    half = len(refs) // 2
    width = refs[0].shape[1] // half
    for shift in range(half):
        target = lax.rem(place_ref[3] + shift, half)
        columns = pl.ds(pl.multiple_of(target * width, LANES), width)
        for row in range(half):
            refs[half + shift][row] = refs[row][:, columns]


def gather_kernel(place_ref, *refs):
    out_ref = refs[-1]
    parts = len(refs) - 1
    for across in range(parts):
        x_from = lax.rem(place_ref[3] + parts - across, parts)
        for down in range(parts):
            y_from = lax.rem(place_ref[2] + parts - down, parts)
            out_ref[y_from * parts + x_from] = refs[across][down]


def split_kernel(place_ref, rows_ref, *out_refs):
    parts = len(out_refs)
    for across, out_ref in enumerate(out_refs):
        x_to = lax.rem(place_ref[3] + across, parts)
        for down in range(parts):
            y_to = lax.rem(place_ref[2] + down, parts)
            out_ref[down] = rows_ref[y_to * parts + x_to]


def turn_out_kernel(place_ref, *refs):
    half = len(refs) // 2
    width = refs[0].shape[2]
    for across in range(half):
        x_from = lax.rem(place_ref[3] + half - across, half)
        columns = pl.ds(pl.multiple_of(x_from * width, LANES), width)
        for down in range(half):
            refs[half + down][:, columns] = refs[across][down]


def columns_kernel(place_ref, *refs):
    out_ref = refs[-1]
    parts = len(refs) - 1
    width = refs[0].shape[1]
    for shift in range(parts):
        source = lax.rem(place_ref[2] + parts - shift, parts)
        out_ref[:, pl.ds(pl.multiple_of(source * width, LANES), width)] = refs[shift][...]


def local_call(kernel, place, arrays, out_shape, name):
    smem = pl.BlockSpec(memory_space=pltpu.SMEM)
    vmem = pl.BlockSpec(memory_space=pltpu.VMEM)
    several = isinstance(out_shape, list)
    return pl.pallas_call(
        kernel,
        in_specs=[smem] + [vmem] * len(arrays),
        out_specs=[vmem] * len(out_shape) if several else vmem,
        out_shape=out_shape,
        compiler_params=pltpu.CompilerParams(vmem_limit_bytes=VMEM_LIMIT),
        name=name,
    )(place, *arrays)


def send_along(arrays, count, along_y):
    moved = [arrays[0]]
    for shift in range(1, count):
        if along_y:
            pairs = [
                (i, (i // count + shift) % count * count + i % count) for i in range(count * count)
            ]
        else:
            pairs = [
                (i, i // count * count + (i % count + shift) % count) for i in range(count * count)
            ]
        moved.append(lax.ppermute(arrays[shift], "tensor", pairs))
    return moved


def cache_row(sessions_ref, owners_ref, slots_ref, slot_count, index):
    session = sessions_ref[index]
    return owners_ref[session] * slot_count + slots_ref[session]


def order_kernel(sessions_ref, owners_ref, slots_ref, in_ref, out_ref, *, slot_count, to_owner):
    def step(index, carry):
        row = cache_row(sessions_ref, owners_ref, slots_ref, slot_count, index)
        if to_owner:
            out_ref[row] = in_ref[index]
        else:
            out_ref[index] = in_ref[row]
        return carry

    lax.fori_loop(0, in_ref.shape[0], step, 0, unroll=8)


def reorder(pieces, sessions, owners, slots, slot_count, to_owner):
    smem = pl.BlockSpec(memory_space=pltpu.SMEM)
    vmem = pl.BlockSpec(memory_space=pltpu.VMEM)
    return pl.pallas_call(
        functools.partial(order_kernel, slot_count=slot_count, to_owner=to_owner),
        in_specs=[smem, smem, smem, vmem],
        out_specs=vmem,
        out_shape=jax.ShapeDtypeStruct(pieces.shape, pieces.dtype),
        compiler_params=pltpu.CompilerParams(vmem_limit_bytes=VMEM_LIMIT),
        name="to_owner_order" if to_owner else "to_group_order",
    )(sessions, owners, slots, pieces)


def token_steps(place_ref, steps_ref, bias_ref, a_log_ref, length, heads):
    f32 = jnp.float32
    lane_from = lax.broadcasted_iota(jnp.int32, (HEADS, LANES), 0)
    lane_to = lax.broadcasted_iota(jnp.int32, (HEADS, LANES), 1)
    chosen = (lane_from == lane_to + place_ref[1] * heads) & (lane_to < heads)
    raw = jnp.dot(steps_ref[...], chosen.astype(jnp.bfloat16), preferred_element_type=f32)
    row_index = lax.broadcasted_iota(jnp.int32, (MAXLEN, LANES), 0)
    shifted = raw + bias_ref[...]
    soft = jnp.maximum(shifted, 0.0) + jnp.log(1.0 + jnp.exp(-jnp.abs(shifted)))
    live = row_index < length
    step = jnp.where(live, soft, 0.0)
    t_index = lax.broadcasted_iota(jnp.int32, (MAXLEN, MAXLEN), 0)
    u_index = lax.broadcasted_iota(jnp.int32, (MAXLEN, MAXLEN), 1)
    causal = t_index >= u_index
    cum = jnp.dot(
        causal.astype(f32),
        step * -jnp.exp(a_log_ref[...]),
        precision=lax.Precision.HIGHEST,
        preferred_element_type=f32,
    )
    return step, cum, live, causal


def spread(columns, first, left):
    one = jnp.broadcast_to(columns[:, first : first + 1], left.shape)
    two = jnp.broadcast_to(columns[:, first + 1 : first + 2], left.shape)
    return jnp.where(left, one, two)


def left_half():
    return lax.broadcasted_iota(jnp.int32, (MAXLEN, LANES), 1) < HEAD_DIM


def tokens_kernel(
    place_ref, sessions_ref, lengths_ref, x_ref, b_ref, c_ref, steps_ref, a_log_ref, bias_ref,
    skip_ref, local_ref, grown_ref, delta_ref, kept_ref, *, heads, slot_count
):
    f32 = jnp.float32
    bf16 = jnp.bfloat16
    half = LANES
    length = lengths_ref[sessions_ref[place_ref[0] * slot_count + pl.program_id(0)]]
    step, cum, live, causal = token_steps(
        place_ref, steps_ref, bias_ref, a_log_ref, length, heads
    )
    last = cum[MAXLEN - 1 : MAXLEN, :]
    to_end = jnp.exp(last - cum) * step
    kept_ref[0] = jnp.broadcast_to(jnp.exp(last), kept_ref.shape[1:])
    drop_rows = (cum - jnp.log(step)).T
    grown_ref[...] = jnp.where(live, jnp.exp(cum), 0.0)
    in_proj = b_ref[...]
    affinity = lax.dot_general(
        c_ref[...], in_proj, (((1,), (1,)), ((), ())), preferred_element_type=f32
    )
    affinity = jnp.where(causal, affinity, 0.0)
    top, low = affinity[:half, :half], affinity[half:, :]
    left = left_half()
    per = delta_ref.shape[2]
    for first in range(0, heads, 2):
        lanes = slice(first * HEAD_DIM, (first + 2) * HEAD_DIM)
        pair = x_ref[:, lanes]
        pair_f32 = pair.astype(f32)
        mixed = []
        for head in (first, first + 1):
            column = cum[:, head : head + 1]
            line = drop_rows[head : head + 1, :]
            w_top = top * jnp.exp(jnp.minimum(column[:half] - line[:, :half], 80.0))
            w_low = low * jnp.exp(jnp.minimum(column[half:] - line, 80.0))
            mixed.append(
                jnp.concatenate(
                    [
                        jnp.dot(w_top.astype(bf16), pair[:half], preferred_element_type=f32),
                        jnp.dot(w_low.astype(bf16), pair, preferred_element_type=f32),
                    ],
                    axis=0,
                )
            )
        out = jnp.where(left, mixed[0], mixed[1]) + skip_ref[:, lanes] * pair_f32
        local_ref[:, lanes] = jnp.where(live, out, 0.0)
        scaled = (pair_f32 * spread(to_end, first, left)).astype(bf16)
        added = lax.dot_general(
            scaled, in_proj, (((0,), (0,)), ((), ())), preferred_element_type=f32
        )
        begin, count = first * HEAD_DIM // per, 2 * HEAD_DIM // per
        delta_ref[begin : begin + count, 0] = added.reshape(count, per, STATE)


def closing_kernel(start_ref, delta_ref, kept_ref, closing_ref, *, heads):
    per = start_ref.shape[2]
    count = HEAD_DIM // per
    for head in range(heads):
        rows = slice(head * count, (head + 1) * count)
        kept = kept_ref[0, :1, head : head + 1].reshape(1, 1, 1)
        closing = kept * start_ref[rows, 0].astype(jnp.float32) + delta_ref[rows, 0]
        closing_ref[rows, 0] = closing.astype(jnp.bfloat16)


def carry_kernel(place_ref, c_ref, start_ref, local_ref, grown_ref, y_ref, *, heads):
    width = heads * HEAD_DIM
    start = start_ref[...].reshape(width, STATE)
    carried = lax.dot_general(
        c_ref[...], start, (((1,), (1,)), ((), ())), preferred_element_type=jnp.float32
    )
    grown = grown_ref[...]
    left = left_half()
    for first in range(0, heads, 2):
        lanes = slice(first * HEAD_DIM, (first + 2) * HEAD_DIM)
        out = local_ref[:, lanes] + spread(grown, first, left) * carried[:, lanes]
        y_ref[:, lanes] = out.astype(jnp.bfloat16)


def session_call(kernel, scalars, slot_count, operands, outputs, flops, name):
    return pl.pallas_call(
        kernel,
        grid_spec=pltpu.PrefetchScalarGridSpec(
            num_scalar_prefetch=len(scalars),
            grid=(slot_count,),
            in_specs=[pl.BlockSpec(block, index) for _, block, index in operands],
            out_specs=[pl.BlockSpec(block, index) for _, block, index in outputs],
        ),
        out_shape=[shape for shape, _, _ in outputs],
        compiler_params=pltpu.CompilerParams(vmem_limit_bytes=VMEM_LIMIT),
        cost_estimate=pl.CostEstimate(
            flops=flops, bytes_accessed=8 * 1024 * 1024, transcendentals=0
        ),
        name=name,
    )(*scalars, *(array for array, _, _ in operands))


def per_device(
    x_in,
    dt_raw,
    b_in,
    c_in,
    a_log,
    dt_bias,
    d_skip,
    state_cache,
    group_sessions,
    owners,
    cache_slots,
    lengths,
):
    tensor_size = lax.axis_size("tensor")
    req_size = lax.axis_size("req")
    slot_count, heads = state_cache.shape[:2]
    per = heads * HEAD_DIM // req_size
    side = tensor_size // GROUPS
    rows = x_in.shape[0]
    width = heads * HEAD_DIM
    bf16 = jnp.bfloat16
    f32 = jnp.float32
    shape = jax.ShapeDtypeStruct
    req_index = lax.axis_index("req")
    tensor_index = lax.axis_index("tensor")
    place = jnp.stack(
        [req_index, tensor_index, tensor_index // side, tensor_index % side]
    ).astype(jnp.int32)
    sessions = group_sessions.reshape(-1)

    pieces = state_cache.reshape(slot_count, req_size, per, STATE)
    held = lax.all_to_all(pieces, "req", split_axis=1, concat_axis=0, tiled=False)
    held = held.reshape(req_size * slot_count, per, STATE)
    held = reorder(held, sessions, owners, cache_slots, slot_count, False)

    proj, *sent = local_call(
        pack_kernel,
        place,
        (x_in, dt_raw, b_in, c_in),
        [shape((rows, 2 * GROUPS * STATE + HEADS), bf16)]
        + [shape((rows, side * width), bf16)] * GROUPS,
        "pack_tokens",
    )
    proj = lax.all_gather(proj, "tensor", axis=0, tiled=True)
    sent = local_call(
        turn_in_kernel,
        place,
        send_along(sent, side, True),
        [shape((GROUPS, rows, width), bf16)] * side,
        "turn_in",
    )
    held, *sent = lax.optimization_barrier((held, *sent))
    start = lax.all_to_all(
        held.reshape(req_size, slot_count, per, STATE), "req", split_axis=0, concat_axis=0
    )
    tokens = local_call(
        gather_kernel,
        place,
        send_along(sent, side, False),
        shape((tensor_size, rows, width), bf16),
        "gather_tokens",
    ).reshape(tensor_size * rows, width)

    pad = ((0, 0), (0, LANES - heads))
    a_row = jnp.pad(a_log[None, :], pad)
    bias_row = jnp.pad(dt_bias[None, :], pad)
    skip_row = jnp.repeat(d_skip, HEAD_DIM)[None, :]
    one_row = lambda j, *_: (0, 0)
    by_session = lambda j, *_: (j, 0)
    x_op = (tokens, (MAXLEN, width), by_session)
    b_op = (proj, (MAXLEN, STATE), lambda j, place, *_: (j, place[2]))
    c_op = (proj, (MAXLEN, STATE), lambda j, place, *_: (j, GROUPS + place[2]))
    steps_op = (proj, (MAXLEN, HEADS), lambda j, *_: (j, 2 * GROUPS))
    a_op = (a_row, (1, LANES), one_row)
    bias_op = (bias_row, (1, LANES), one_row)
    skip_op = (skip_row, (1, width), one_row)
    scalars = (place, sessions, lengths)
    sizes = dict(heads=heads, slot_count=slot_count)
    piece_block = (req_size, 1, per, STATE)
    by_slot = lambda j, *_: (0, j, 0, 0)
    total_rows = tensor_size * rows

    state_shape = (req_size, slot_count, per, STATE)
    kept_block = ((1, 8, LANES), lambda j, *_: (j, 0, 0))
    local, grown, delta, kept = session_call(
        functools.partial(tokens_kernel, **sizes),
        scalars,
        slot_count,
        [x_op, b_op, c_op, steps_op, a_op, bias_op, skip_op],
        [
            (shape((total_rows, width), f32), (MAXLEN, width), by_session),
            (shape((total_rows, LANES), f32), (MAXLEN, LANES), by_session),
            (shape(state_shape, f32), piece_block, by_slot),
            (shape((slot_count, 8, LANES), f32), *kept_block),
        ],
        10_000_000_000,
        "tokens_part",
    )

    (closing,) = session_call(
        functools.partial(closing_kernel, heads=heads),
        (),
        slot_count,
        [(start, piece_block, by_slot), (delta, piece_block, by_slot), (kept, *kept_block)],
        [(shape(state_shape, bf16), piece_block, by_slot)],
        1_000_000_000,
        "closing_states",
    )
    closing, start = lax.optimization_barrier((closing, start))
    back = lax.all_to_all(closing, "req", split_axis=0, concat_axis=0)
    back = back.reshape(req_size * slot_count, per, STATE)
    back = reorder(back, sessions, owners, cache_slots, slot_count, True)

    (mixed,) = session_call(
        functools.partial(carry_kernel, heads=heads),
        (place,),
        slot_count,
        [
            c_op,
            (start, piece_block, by_slot),
            (local, (MAXLEN, width), by_session),
            (grown, (MAXLEN, LANES), by_session),
        ],
        [(shape((total_rows, width), bf16), (MAXLEN, width), by_session)],
        3_000_000_000,
        "carried_part",
    )
    sent = local_call(
        split_kernel,
        place,
        (mixed.reshape(tensor_size, rows, width),),
        [shape((GROUPS, rows, width), bf16)] * side,
        "split_rows",
    )
    sent = local_call(
        turn_out_kernel,
        place,
        send_along(sent, side, False),
        [shape((rows, side * width), bf16)] * GROUPS,
        "turn_out",
    )
    back, *sent = lax.optimization_barrier((back, *sent))
    back = lax.all_to_all(
        back.reshape(req_size, slot_count, per, STATE), "req", split_axis=0, concat_axis=0
    )
    new_cache = back.transpose(1, 0, 2, 3).reshape(state_cache.shape)
    y_out = local_call(
        columns_kernel,
        place,
        send_along(sent, side, True),
        shape(x_in.shape, bf16),
        "join_columns",
    )
    return y_out, new_cache


def solution(mesh):
    tokens = P(("req", "tensor"), None)
    states = P("req", "tensor", None, None)
    placed = (tokens,) * 4 + (P("tensor"),) * 3 + (states,) + (P(),) * 4
    return jax.shard_map(
        per_device,
        mesh=mesh,
        in_specs=placed,
        out_specs=(tokens, states),
        check_vma=False,
    )
```

```python
import functools

import jax
import jax.numpy as jnp
from jax import lax
from jax.experimental import pallas as pl
from jax.experimental.pallas import tpu as pltpu
from jax.sharding import PartitionSpec as P

HEADS = 128
HEAD_DIM = 64
STATE = 128
GROUPS = 4
MAXLEN = 192
LANES = 128
VMEM_LIMIT = 48 * 1024 * 1024


def pack_kernel(place_ref, x_ref, dt_ref, b_ref, c_ref, *out_refs):
    parts = len(out_refs)
    width = x_ref.shape[1] // parts
    for shift, out_ref in enumerate(out_refs):
        target = lax.rem(place_ref[2] + shift, parts)
        group = pl.ds(pl.multiple_of(target * STATE, LANES), STATE)
        out_ref[:, :width] = x_ref[:, pl.ds(pl.multiple_of(target * width, LANES), width)]
        out_ref[:, width : width + STATE] = b_ref[:, group]
        out_ref[:, width + STATE : width + 2 * STATE] = c_ref[:, group]
        out_ref[:, width + 2 * STATE :] = dt_ref[...]


def turn_in_kernel(place_ref, *refs):
    half = len(refs) // 2
    extra = 2 * STATE + HEADS
    width = (refs[0].shape[1] - extra) // half
    for shift in range(half):
        target = lax.rem(place_ref[3] + shift, half)
        columns = pl.ds(pl.multiple_of(target * width, LANES), width)
        for row in range(half):
            refs[half + shift][row, :, :width] = refs[row][:, columns]
            refs[half + shift][row, :, width:] = refs[row][:, half * width :]


def gather_kernel(place_ref, *refs):
    out_ref = refs[-1]
    parts = len(refs) - 1
    for across in range(parts):
        x_from = lax.rem(place_ref[3] + parts - across, parts)
        for down in range(parts):
            y_from = lax.rem(place_ref[2] + parts - down, parts)
            out_ref[y_from * parts + x_from] = refs[across][down]


def split_kernel(place_ref, rows_ref, *out_refs):
    parts = len(out_refs)
    for across, out_ref in enumerate(out_refs):
        x_to = lax.rem(place_ref[3] + across, parts)
        for down in range(parts):
            y_to = lax.rem(place_ref[2] + down, parts)
            out_ref[down] = rows_ref[y_to * parts + x_to]


def turn_out_kernel(place_ref, *refs):
    half = len(refs) // 2
    width = refs[0].shape[2]
    for across in range(half):
        x_from = lax.rem(place_ref[3] + half - across, half)
        columns = pl.ds(pl.multiple_of(x_from * width, LANES), width)
        for down in range(half):
            refs[half + down][:, columns] = refs[across][down]


def columns_kernel(place_ref, *refs):
    out_ref = refs[-1]
    parts = len(refs) - 1
    width = refs[0].shape[1]
    for shift in range(parts):
        source = lax.rem(place_ref[2] + parts - shift, parts)
        out_ref[:, pl.ds(pl.multiple_of(source * width, LANES), width)] = refs[shift][...]


def local_call(kernel, place, arrays, out_shape, name):
    smem = pl.BlockSpec(memory_space=pltpu.SMEM)
    vmem = pl.BlockSpec(memory_space=pltpu.VMEM)
    several = isinstance(out_shape, list)
    return pl.pallas_call(
        kernel,
        in_specs=[smem] + [vmem] * len(arrays),
        out_specs=[vmem] * len(out_shape) if several else vmem,
        out_shape=out_shape,
        compiler_params=pltpu.CompilerParams(vmem_limit_bytes=VMEM_LIMIT),
        name=name,
    )(place, *arrays)


def send_along(arrays, count, along_y):
    moved = list(arrays)
    for shift in sorted(range(1, count), key=lambda d: -min(d, count - d)):
        if along_y:
            pairs = [
                (i, (i // count + shift) % count * count + i % count) for i in range(count * count)
            ]
        else:
            pairs = [
                (i, i // count * count + (i % count + shift) % count) for i in range(count * count)
            ]
        moved[shift] = lax.ppermute(arrays[shift], "tensor", pairs)
    return moved


def member_at(spot, count):
    chips = count // 2
    return lax.rem(lax.rem(spot, chips) * 5, chips) * 2 + spot // chips


def spot_of(member, count):
    chips = count // 2
    return lax.rem(member, 2) * chips + lax.rem(member // 2 * 13, chips)


def members(count):
    chips = count // 2
    return [spot % chips * 5 % chips * 2 + spot // chips for spot in range(count)]


def rows_kernel(sessions_ref, owners_ref, slots_ref, rows_ref, *, slot_count):
    count = rows_ref.shape[0] // slot_count

    def step(spot, carry):
        group = member_at(spot, count)
        for slot in range(slot_count):
            session = sessions_ref[group * slot_count + slot]
            owner = spot_of(owners_ref[session], count)
            rows_ref[spot * slot_count + slot] = owner * slot_count + slots_ref[session]
        return carry

    lax.fori_loop(0, count, step, 0)


def cache_rows(sessions, owners, slots, slot_count):
    smem = pl.BlockSpec(memory_space=pltpu.SMEM)
    return pl.pallas_call(
        functools.partial(rows_kernel, slot_count=slot_count),
        in_specs=[smem] * 3,
        out_specs=smem,
        out_shape=jax.ShapeDtypeStruct(sessions.shape, jnp.int32),
        name="cache_rows",
    )(sessions, owners, slots)


def order_kernel(rows_ref, in_ref, out_ref, *, to_owner):
    def step(index, carry):
        row = rows_ref[index]
        if to_owner:
            out_ref[row] = in_ref[index]
        else:
            out_ref[index] = in_ref[row]
        return carry

    lax.fori_loop(0, in_ref.shape[0], step, 0, unroll=16)


def reorder(pieces, rows, to_owner):
    smem = pl.BlockSpec(memory_space=pltpu.SMEM)
    vmem = pl.BlockSpec(memory_space=pltpu.VMEM)
    return pl.pallas_call(
        functools.partial(order_kernel, to_owner=to_owner),
        in_specs=[smem, vmem],
        out_specs=vmem,
        out_shape=jax.ShapeDtypeStruct(pieces.shape, pieces.dtype),
        compiler_params=pltpu.CompilerParams(vmem_limit_bytes=VMEM_LIMIT),
        name="to_owner_order" if to_owner else "to_group_order",
    )(rows, pieces)


def exchange(states, axis_size, split_axis=0):
    return lax.all_to_all(
        states, "req", split_axis=split_axis, concat_axis=0, axis_index_groups=[members(axis_size)]
    )


def token_steps(place_ref, steps_ref, bias_ref, a_log_ref, length, heads):
    f32 = jnp.float32
    lane_from = lax.broadcasted_iota(jnp.int32, (HEADS, LANES), 0)
    lane_to = lax.broadcasted_iota(jnp.int32, (HEADS, LANES), 1)
    chosen = (lane_from == lane_to + place_ref[1] * heads) & (lane_to < heads)
    raw = jnp.dot(steps_ref[...], chosen.astype(jnp.bfloat16), preferred_element_type=f32)
    row_index = lax.broadcasted_iota(jnp.int32, (MAXLEN, LANES), 0)
    shifted = raw + bias_ref[...]
    soft = jnp.maximum(shifted, 0.0) + jnp.log(1.0 + jnp.exp(-jnp.abs(shifted)))
    live = row_index < length
    step = jnp.where(live, soft, 0.0)
    t_index = lax.broadcasted_iota(jnp.int32, (MAXLEN, MAXLEN), 0)
    u_index = lax.broadcasted_iota(jnp.int32, (MAXLEN, MAXLEN), 1)
    causal = t_index >= u_index
    cum = jnp.dot(
        causal.astype(f32),
        step * -jnp.exp(a_log_ref[...]),
        precision=lax.Precision.HIGHEST,
        preferred_element_type=f32,
    )
    return step, cum, live, causal


def spread(columns, first, left):
    one = jnp.broadcast_to(columns[:, first : first + 1], left.shape)
    two = jnp.broadcast_to(columns[:, first + 1 : first + 2], left.shape)
    return jnp.where(left, one, two)


def left_half():
    return lax.broadcasted_iota(jnp.int32, (MAXLEN, LANES), 1) < HEAD_DIM


def tokens_kernel(
    place_ref, sessions_ref, lengths_ref, x_ref, b_ref, c_ref, steps_ref, a_log_ref, bias_ref,
    skip_ref, local_ref, grown_ref, delta_ref, kept_ref, *, heads, slot_count
):
    f32 = jnp.float32
    bf16 = jnp.bfloat16
    half = LANES
    length = lengths_ref[sessions_ref[place_ref[0] * slot_count + pl.program_id(0)]]
    step, cum, live, causal = token_steps(
        place_ref, steps_ref, bias_ref, a_log_ref, length, heads
    )
    last = cum[MAXLEN - 1 : MAXLEN, :]
    to_end = jnp.exp(last - cum) * step
    kept_ref[0] = jnp.broadcast_to(jnp.exp(last), kept_ref.shape[1:])
    drop_rows = (cum - jnp.log(step)).T
    grown_ref[...] = jnp.where(live, jnp.exp(cum), 0.0)
    in_proj = b_ref[...]
    affinity = lax.dot_general(
        c_ref[...], in_proj, (((1,), (1,)), ((), ())), preferred_element_type=f32
    )
    affinity = jnp.where(causal, affinity, 0.0)
    top, low = affinity[:half, :half], affinity[half:, :]
    left = left_half()
    per = delta_ref.shape[2]
    for first in range(0, heads, 2):
        lanes = slice(first * HEAD_DIM, (first + 2) * HEAD_DIM)
        pair = x_ref[:, lanes]
        pair_f32 = pair.astype(f32)
        mixed = []
        for head in (first, first + 1):
            column = cum[:, head : head + 1]
            line = drop_rows[head : head + 1, :]
            w_top = top * jnp.exp(jnp.minimum(column[:half] - line[:, :half], 80.0))
            w_low = low * jnp.exp(jnp.minimum(column[half:] - line, 80.0))
            mixed.append(
                jnp.concatenate(
                    [
                        jnp.dot(w_top.astype(bf16), pair[:half], preferred_element_type=f32),
                        jnp.dot(w_low.astype(bf16), pair, preferred_element_type=f32),
                    ],
                    axis=0,
                )
            )
        out = jnp.where(left, mixed[0], mixed[1]) + skip_ref[:, lanes] * pair_f32
        local_ref[:, lanes] = jnp.where(live, out, 0.0)
        scaled = (pair_f32 * spread(to_end, first, left)).astype(bf16)
        added = lax.dot_general(
            scaled, in_proj, (((0,), (0,)), ((), ())), preferred_element_type=f32
        )
        begin, count = first * HEAD_DIM // per, 2 * HEAD_DIM // per
        delta_ref[begin : begin + count, 0] = added.reshape(count, per, STATE)


def closing_kernel(start_ref, delta_ref, kept_ref, closing_ref, *, heads):
    per = start_ref.shape[2]
    count = HEAD_DIM // per
    for head in range(heads):
        rows = slice(head * count, (head + 1) * count)
        kept = kept_ref[0, :1, head : head + 1].reshape(1, 1, 1)
        closing = kept * start_ref[rows, 0].astype(jnp.float32) + delta_ref[rows, 0]
        closing_ref[rows, 0] = closing.astype(jnp.bfloat16)


def carry_kernel(place_ref, c_ref, start_ref, local_ref, grown_ref, y_ref, *, heads):
    width = heads * HEAD_DIM
    start = start_ref[...].reshape(width, STATE)
    carried = lax.dot_general(
        c_ref[...], start, (((1,), (1,)), ((), ())), preferred_element_type=jnp.float32
    )
    grown = grown_ref[...]
    left = left_half()
    for first in range(0, heads, 2):
        lanes = slice(first * HEAD_DIM, (first + 2) * HEAD_DIM)
        out = local_ref[:, lanes] + spread(grown, first, left) * carried[:, lanes]
        y_ref[:, lanes] = out.astype(jnp.bfloat16)


def session_call(kernel, scalars, slot_count, operands, outputs, flops, name):
    return pl.pallas_call(
        kernel,
        grid_spec=pltpu.PrefetchScalarGridSpec(
            num_scalar_prefetch=len(scalars),
            grid=(slot_count,),
            in_specs=[pl.BlockSpec(block, index) for _, block, index in operands],
            out_specs=[pl.BlockSpec(block, index) for _, block, index in outputs],
        ),
        out_shape=[shape for shape, _, _ in outputs],
        compiler_params=pltpu.CompilerParams(vmem_limit_bytes=VMEM_LIMIT),
        cost_estimate=pl.CostEstimate(
            flops=flops, bytes_accessed=8 * 1024 * 1024, transcendentals=0
        ),
        name=name,
    )(*scalars, *(array for array, _, _ in operands))


def per_device(
    x_in,
    dt_raw,
    b_in,
    c_in,
    a_log,
    dt_bias,
    d_skip,
    state_cache,
    group_sessions,
    owners,
    cache_slots,
    lengths,
):
    tensor_size = lax.axis_size("tensor")
    req_size = lax.axis_size("req")
    slot_count, heads = state_cache.shape[:2]
    per = heads * HEAD_DIM // req_size
    side = tensor_size // GROUPS
    rows = x_in.shape[0]
    width = heads * HEAD_DIM
    bf16 = jnp.bfloat16
    f32 = jnp.float32
    shape = jax.ShapeDtypeStruct
    req_index = lax.axis_index("req")
    tensor_index = lax.axis_index("tensor")
    place = jnp.stack(
        [req_index, tensor_index, tensor_index // side, tensor_index % side]
    ).astype(jnp.int32)
    sessions = group_sessions.reshape(-1)

    state_shape = (req_size, slot_count, per, STATE)
    table = cache_rows(sessions, owners, cache_slots, slot_count)
    pieces = state_cache.reshape(slot_count, req_size, per, STATE)
    held = exchange(pieces, req_size, 1).reshape(req_size * slot_count, per, STATE)
    held = reorder(held, table, False)

    extra = 2 * STATE + HEADS
    sent = local_call(
        pack_kernel,
        place,
        (x_in, dt_raw, b_in, c_in),
        [shape((rows, side * width + extra), bf16)] * GROUPS,
        "pack_tokens",
    )
    sent = local_call(
        turn_in_kernel,
        place,
        send_along(sent, side, True),
        [shape((GROUPS, rows, width + extra), bf16)] * side,
        "turn_in",
    )
    sent = send_along(sent, side, False)
    held, sent[side // 2] = lax.optimization_barrier((held, sent[side // 2]))
    start = exchange(held.reshape(state_shape), req_size)
    packed = local_call(
        gather_kernel,
        place,
        sent,
        shape((tensor_size, rows, width + extra), bf16),
        "gather_tokens",
    ).reshape(tensor_size * rows, width + extra)

    pad = ((0, 0), (0, LANES - heads))
    a_row = jnp.pad(a_log[None, :], pad)
    bias_row = jnp.pad(dt_bias[None, :], pad)
    skip_row = jnp.repeat(d_skip, HEAD_DIM)[None, :]
    one_row = lambda j, *_: (0, 0)
    by_session = lambda j, *_: (j, 0)
    x_op = (packed, (MAXLEN, width), by_session)
    b_op = (packed, (MAXLEN, STATE), lambda j, *_: (j, width // STATE))
    c_op = (packed, (MAXLEN, STATE), lambda j, *_: (j, width // STATE + 1))
    steps_op = (packed, (MAXLEN, HEADS), lambda j, *_: (j, width // STATE + 2))
    a_op = (a_row, (1, LANES), one_row)
    bias_op = (bias_row, (1, LANES), one_row)
    skip_op = (skip_row, (1, width), one_row)
    scalars = (place, sessions, lengths)
    sizes = dict(heads=heads, slot_count=slot_count)
    piece_block = (req_size, 1, per, STATE)
    by_slot = lambda j, *_: (0, j, 0, 0)
    total_rows = tensor_size * rows

    kept_block = ((1, 8, LANES), lambda j, *_: (j, 0, 0))
    local, grown, delta, kept = session_call(
        functools.partial(tokens_kernel, **sizes),
        scalars,
        slot_count,
        [x_op, b_op, c_op, steps_op, a_op, bias_op, skip_op],
        [
            (shape((total_rows, width), f32), (MAXLEN, width), by_session),
            (shape((total_rows, LANES), f32), (MAXLEN, LANES), by_session),
            (shape(state_shape, f32), piece_block, by_slot),
            (shape((slot_count, 8, LANES), f32), *kept_block),
        ],
        10_000_000_000,
        "tokens_part",
    )

    (closing,) = session_call(
        functools.partial(closing_kernel, heads=heads),
        (),
        slot_count,
        [(start, piece_block, by_slot), (delta, piece_block, by_slot), (kept, *kept_block)],
        [(shape(state_shape, bf16), piece_block, by_slot)],
        1_000_000_000,
        "closing_states",
    )
    closing, start = lax.optimization_barrier((closing, start))
    back = exchange(closing, req_size).reshape(req_size * slot_count, per, STATE)
    back = reorder(back, table, True)

    (mixed,) = session_call(
        functools.partial(carry_kernel, heads=heads),
        (place,),
        slot_count,
        [
            c_op,
            (start, piece_block, by_slot),
            (local, (MAXLEN, width), by_session),
            (grown, (MAXLEN, LANES), by_session),
        ],
        [(shape((total_rows, width), bf16), (MAXLEN, width), by_session)],
        3_000_000_000,
        "carried_part",
    )
    sent = local_call(
        split_kernel,
        place,
        (mixed.reshape(tensor_size, rows, width),),
        [shape((GROUPS, rows, width), bf16)] * side,
        "split_rows",
    )
    sent = local_call(
        turn_out_kernel,
        place,
        send_along(sent, side, False),
        [shape((rows, side * width), bf16)] * GROUPS,
        "turn_out",
    )
    back, *sent = lax.optimization_barrier((back, *sent))
    back = exchange(back.reshape(state_shape), req_size)
    new_cache = back.transpose(1, 0, 2, 3).reshape(state_cache.shape)
    y_out = local_call(
        columns_kernel,
        place,
        send_along(sent, side, True),
        shape(x_in.shape, bf16),
        "join_columns",
    )
    return y_out, new_cache


def solution(mesh):
    tokens = P(("req", "tensor"), None)
    states = P("req", "tensor", None, None)
    placed = (tokens,) * 4 + (P("tensor"),) * 3 + (states,) + (P(),) * 4
    return jax.shard_map(
        per_device,
        mesh=mesh,
        in_specs=placed,
        out_specs=(tokens, states),
        check_vma=False,
    )
```

```python
import functools

import jax
import jax.numpy as jnp
from jax import lax
from jax.experimental import pallas as pl
from jax.experimental.pallas import tpu as pltpu
from jax.sharding import PartitionSpec as P

HEADS = 128
HEAD_DIM = 64
STATE = 128
GROUPS = 4
MAXLEN = 192
LANES = 128
VMEM_LIMIT = 20 * 1024 * 1024


def pack_kernel(place_ref, x_ref, dt_ref, b_ref, c_ref, *out_refs):
    parts = len(out_refs)
    side = parts // GROUPS
    width = x_ref.shape[1] // parts
    for shift, out_ref in enumerate(out_refs):
        y_to = lax.rem(place_ref[2] + shift // side, GROUPS)
        x_to = lax.rem(place_ref[3] + shift % side, side)
        columns = pl.ds(pl.multiple_of((y_to * side + x_to) * width, LANES), width)
        group = pl.ds(pl.multiple_of(y_to * STATE, LANES), STATE)
        out_ref[:, :width] = x_ref[:, columns]
        out_ref[:, width : width + STATE] = b_ref[:, group]
        out_ref[:, width + STATE : width + 2 * STATE] = c_ref[:, group]
        out_ref[:, width + 2 * STATE :] = dt_ref[...]


def gather_kernel(place_ref, *refs):
    out_ref = refs[-1]
    side = (len(refs) - 1) // GROUPS
    for shift in range(len(refs) - 1):
        y_from = lax.rem(place_ref[2] + GROUPS - shift // side, GROUPS)
        x_from = lax.rem(place_ref[3] + side - shift % side, side)
        out_ref[y_from * side + x_from] = refs[shift][...]


def split_kernel(place_ref, rows_ref, *out_refs):
    parts = len(out_refs)
    for across, out_ref in enumerate(out_refs):
        x_to = lax.rem(place_ref[3] + across, parts)
        for down in range(parts):
            y_to = lax.rem(place_ref[2] + down, parts)
            out_ref[down] = rows_ref[y_to * parts + x_to]


def turn_out_kernel(place_ref, *refs):
    half = len(refs) // 2
    width = refs[0].shape[2]
    for across in range(half):
        x_from = lax.rem(place_ref[3] + half - across, half)
        columns = pl.ds(pl.multiple_of(x_from * width, LANES), width)
        for down in range(half):
            refs[half + down][:, columns] = refs[across][down]


def columns_kernel(place_ref, *refs):
    out_ref = refs[-1]
    parts = len(refs) - 1
    width = refs[0].shape[1]
    for shift in range(parts):
        source = lax.rem(place_ref[2] + parts - shift, parts)
        out_ref[:, pl.ds(pl.multiple_of(source * width, LANES), width)] = refs[shift][...]


def local_call(kernel, place, arrays, out_shape, name):
    smem = pl.BlockSpec(memory_space=pltpu.SMEM)
    vmem = pl.BlockSpec(memory_space=pltpu.VMEM)
    several = isinstance(out_shape, list)
    return pl.pallas_call(
        kernel,
        in_specs=[smem] + [vmem] * len(arrays),
        out_specs=[vmem] * len(out_shape) if several else vmem,
        out_shape=out_shape,
        compiler_params=pltpu.CompilerParams(vmem_limit_bytes=VMEM_LIMIT),
        name=name,
    )(place, *arrays)


def moved_by(count, down, across):
    return [
        (i, (i // count + down) % count * count + (i % count + across) % count)
        for i in range(count * count)
    ]


def send_along(arrays, count, along_y):
    moved = list(arrays)
    for shift in sorted(range(1, count), key=lambda d: -min(d, count - d)):
        pairs = moved_by(count, shift, 0) if along_y else moved_by(count, 0, shift)
        moved[shift] = lax.ppermute(arrays[shift], "tensor", pairs)
    return moved


def member_at(spot, count):
    chips = count // 2
    return lax.rem(lax.rem(spot, chips) * 7, chips) * 2 + spot // chips


def spot_of(member, count):
    chips = count // 2
    return lax.rem(member, 2) * chips + lax.rem(member // 2 * 7, chips)


def members(count):
    chips = count // 2
    return [spot % chips * 7 % chips * 2 + spot // chips for spot in range(count)]


def rows_kernel(sessions_ref, owners_ref, slots_ref, rows_ref, *, slot_count):
    count = rows_ref.shape[0] // slot_count

    def step(spot, carry):
        group = member_at(spot, count)
        for slot in range(slot_count):
            session = sessions_ref[group * slot_count + slot]
            owner = spot_of(owners_ref[session], count)
            rows_ref[spot * slot_count + slot] = owner * slot_count + slots_ref[session]
        return carry

    lax.fori_loop(0, count, step, 0)


def cache_rows(sessions, owners, slots, slot_count):
    smem = pl.BlockSpec(memory_space=pltpu.SMEM)
    return pl.pallas_call(
        functools.partial(rows_kernel, slot_count=slot_count),
        in_specs=[smem] * 3,
        out_specs=smem,
        out_shape=jax.ShapeDtypeStruct(sessions.shape, jnp.int32),
        name="cache_rows",
    )(sessions, owners, slots)


def order_kernel(rows_ref, in_ref, out_ref, *, to_owner):
    def step(index, carry):
        row = rows_ref[index]
        if to_owner:
            out_ref[row] = in_ref[index]
        else:
            out_ref[index] = in_ref[row]
        return carry

    lax.fori_loop(0, in_ref.shape[0], step, 0, unroll=16)


def reorder(pieces, rows, to_owner):
    smem = pl.BlockSpec(memory_space=pltpu.SMEM)
    vmem = pl.BlockSpec(memory_space=pltpu.VMEM)
    return pl.pallas_call(
        functools.partial(order_kernel, to_owner=to_owner),
        in_specs=[smem, vmem],
        out_specs=vmem,
        out_shape=jax.ShapeDtypeStruct(pieces.shape, pieces.dtype),
        compiler_params=pltpu.CompilerParams(vmem_limit_bytes=VMEM_LIMIT),
        name="to_owner_order" if to_owner else "to_group_order",
    )(rows, pieces)


def exchange(states, axis_size, split_axis=0):
    return lax.all_to_all(
        states, "req", split_axis=split_axis, concat_axis=0, axis_index_groups=[members(axis_size)]
    )


def token_steps(place_ref, steps_ref, bias_ref, a_log_ref, length, heads):
    f32 = jnp.float32
    lane_from = lax.broadcasted_iota(jnp.int32, (HEADS, LANES), 0)
    lane_to = lax.broadcasted_iota(jnp.int32, (HEADS, LANES), 1)
    chosen = (lane_from == lane_to + place_ref[1] * heads) & (lane_to < heads)
    raw = jnp.dot(steps_ref[...], chosen.astype(jnp.bfloat16), preferred_element_type=f32)
    row_index = lax.broadcasted_iota(jnp.int32, (MAXLEN, LANES), 0)
    shifted = raw + bias_ref[...]
    soft = jnp.maximum(shifted, 0.0) + jnp.log(1.0 + jnp.exp(-jnp.abs(shifted)))
    live = row_index < length
    step = jnp.where(live, soft, 0.0)
    t_index = lax.broadcasted_iota(jnp.int32, (MAXLEN, MAXLEN), 0)
    u_index = lax.broadcasted_iota(jnp.int32, (MAXLEN, MAXLEN), 1)
    causal = t_index >= u_index
    cum = jnp.dot(
        causal.astype(f32),
        step * -jnp.exp(a_log_ref[...]),
        precision=lax.Precision.HIGHEST,
        preferred_element_type=f32,
    )
    return step, cum, live, causal


def spread(columns, first, left):
    one = jnp.broadcast_to(columns[:, first : first + 1], left.shape)
    two = jnp.broadcast_to(columns[:, first + 1 : first + 2], left.shape)
    return jnp.where(left, one, two)


def left_half():
    return lax.broadcasted_iota(jnp.int32, (MAXLEN, LANES), 1) < HEAD_DIM


def delta_kernel(
    place_ref, sessions_ref, lengths_ref, x_ref, b_ref, steps_ref, a_log_ref, bias_ref,
    delta_ref, kept_ref, *, heads, slot_count
):
    length = lengths_ref[sessions_ref[place_ref[0] * slot_count + pl.program_id(0)]]
    step, cum, _, _ = token_steps(place_ref, steps_ref, bias_ref, a_log_ref, length, heads)
    last = cum[MAXLEN - 1 : MAXLEN, :]
    to_end = jnp.exp(last - cum) * step
    kept_ref[0] = jnp.broadcast_to(jnp.exp(last), kept_ref.shape[1:])
    left = left_half()
    in_proj = b_ref[...]
    per = delta_ref.shape[2]
    for first in range(0, heads, 2):
        lanes = slice(first * HEAD_DIM, (first + 2) * HEAD_DIM)
        scaled = x_ref[:, lanes].astype(jnp.float32) * spread(to_end, first, left)
        added = lax.dot_general(
            scaled.astype(jnp.bfloat16),
            in_proj,
            (((0,), (0,)), ((), ())),
            preferred_element_type=jnp.float32,
        )
        begin, count = first * HEAD_DIM // per, 2 * HEAD_DIM // per
        delta_ref[begin : begin + count, 0] = added.reshape(count, per, STATE)


def closing_kernel(start_ref, delta_ref, kept_ref, closing_ref, *, heads):
    per = start_ref.shape[2]
    count = HEAD_DIM // per
    for head in range(heads):
        rows = slice(head * count, (head + 1) * count)
        kept = kept_ref[0, :1, head : head + 1].reshape(1, 1, 1)
        closing = kept * start_ref[rows, 0].astype(jnp.float32) + delta_ref[rows, 0]
        closing_ref[rows, 0] = closing.astype(jnp.bfloat16)


def outputs_kernel(
    place_ref, sessions_ref, lengths_ref, x_ref, b_ref, c_ref, steps_ref, start_ref, a_log_ref,
    bias_ref, skip_ref, y_ref, *, heads, slot_count
):
    f32 = jnp.float32
    bf16 = jnp.bfloat16
    half = LANES
    width = heads * HEAD_DIM
    length = lengths_ref[sessions_ref[place_ref[0] * slot_count + pl.program_id(0)]]
    step, cum, live, causal = token_steps(
        place_ref, steps_ref, bias_ref, a_log_ref, length, heads
    )
    drop_rows = (cum - jnp.log(step)).T
    grown = jnp.exp(cum)
    out_proj = c_ref[...]
    affinity = lax.dot_general(
        out_proj, b_ref[...], (((1,), (1,)), ((), ())), preferred_element_type=f32
    )
    affinity = jnp.where(causal, affinity, 0.0)
    top, low = affinity[:half, :half], affinity[half:, :]
    carried = lax.dot_general(
        out_proj,
        start_ref[...].reshape(width, STATE),
        (((1,), (1,)), ((), ())),
        preferred_element_type=f32,
    )
    left = left_half()
    for first in range(0, heads, 2):
        lanes = slice(first * HEAD_DIM, (first + 2) * HEAD_DIM)
        pair = x_ref[:, lanes]
        mixed = []
        for head in (first, first + 1):
            column = cum[:, head : head + 1]
            line = drop_rows[head : head + 1, :]
            w_top = top * jnp.exp(jnp.minimum(column[:half] - line[:, :half], 80.0))
            w_low = low * jnp.exp(jnp.minimum(column[half:] - line, 80.0))
            mixed.append(
                jnp.concatenate(
                    [
                        jnp.dot(w_top.astype(bf16), pair[:half], preferred_element_type=f32),
                        jnp.dot(w_low.astype(bf16), pair, preferred_element_type=f32),
                    ],
                    axis=0,
                )
            )
        out = (
            jnp.where(left, mixed[0], mixed[1])
            + spread(grown, first, left) * carried[:, lanes]
            + skip_ref[:, lanes] * pair.astype(f32)
        )
        y_ref[:, lanes] = jnp.where(live, out, 0.0).astype(bf16)


def session_call(kernel, scalars, slot_count, operands, outputs, flops, name):
    return pl.pallas_call(
        kernel,
        grid_spec=pltpu.PrefetchScalarGridSpec(
            num_scalar_prefetch=len(scalars),
            grid=(slot_count,),
            in_specs=[pl.BlockSpec(block, index) for _, block, index in operands],
            out_specs=[pl.BlockSpec(block, index) for _, block, index in outputs],
        ),
        out_shape=[shape for shape, _, _ in outputs],
        compiler_params=pltpu.CompilerParams(vmem_limit_bytes=VMEM_LIMIT),
        cost_estimate=pl.CostEstimate(
            flops=flops, bytes_accessed=8 * 1024 * 1024, transcendentals=0
        ),
        name=name,
    )(*scalars, *(array for array, _, _ in operands))


def per_device(
    x_in,
    dt_raw,
    b_in,
    c_in,
    a_log,
    dt_bias,
    d_skip,
    state_cache,
    group_sessions,
    owners,
    cache_slots,
    lengths,
):
    tensor_size = lax.axis_size("tensor")
    req_size = lax.axis_size("req")
    slot_count, heads = state_cache.shape[:2]
    per = heads * HEAD_DIM // req_size
    side = tensor_size // GROUPS
    rows = x_in.shape[0]
    width = heads * HEAD_DIM
    bf16 = jnp.bfloat16
    f32 = jnp.float32
    shape = jax.ShapeDtypeStruct
    req_index = lax.axis_index("req")
    tensor_index = lax.axis_index("tensor")
    place = jnp.stack(
        [req_index, tensor_index, tensor_index // side, tensor_index % side]
    ).astype(jnp.int32)
    sessions = group_sessions.reshape(-1)

    state_shape = (req_size, slot_count, per, STATE)
    table = cache_rows(sessions, owners, cache_slots, slot_count)
    pieces = state_cache.reshape(slot_count, req_size, per, STATE)
    held = exchange(pieces, req_size, 1).reshape(req_size * slot_count, per, STATE)
    held = reorder(held, table, False)

    extra = 2 * STATE + HEADS
    piece = shape((rows, width + extra), bf16)
    sent = local_call(
        pack_kernel, place, (x_in, dt_raw, b_in, c_in), [piece] * tensor_size, "pack_tokens"
    )
    sent = list(sent)
    for shift in range(1, tensor_size):
        pairs = moved_by(side, shift // side, shift % side)
        sent[shift] = lax.ppermute(sent[shift], "tensor", pairs)
    early = tensor_size // 2 + 1
    held, *sent[:early] = lax.optimization_barrier((held, *sent[:early]))
    start = exchange(held.reshape(state_shape), req_size)
    packed = local_call(
        gather_kernel,
        place,
        sent,
        shape((tensor_size, rows, width + extra), bf16),
        "gather_tokens",
    ).reshape(tensor_size * rows, width + extra)

    pad = ((0, 0), (0, LANES - heads))
    a_row = jnp.pad(a_log[None, :], pad)
    bias_row = jnp.pad(dt_bias[None, :], pad)
    skip_row = jnp.repeat(d_skip, HEAD_DIM)[None, :]
    one_row = lambda j, *_: (0, 0)
    by_session = lambda j, *_: (j, 0)
    x_op = (packed, (MAXLEN, width), by_session)
    b_op = (packed, (MAXLEN, STATE), lambda j, *_: (j, width // STATE))
    c_op = (packed, (MAXLEN, STATE), lambda j, *_: (j, width // STATE + 1))
    steps_op = (packed, (MAXLEN, HEADS), lambda j, *_: (j, width // STATE + 2))
    a_op = (a_row, (1, LANES), one_row)
    bias_op = (bias_row, (1, LANES), one_row)
    skip_op = (skip_row, (1, width), one_row)
    scalars = (place, sessions, lengths)
    sizes = dict(heads=heads, slot_count=slot_count)
    piece_block = (req_size, 1, per, STATE)
    by_slot = lambda j, *_: (0, j, 0, 0)
    total_rows = tensor_size * rows

    kept_block = ((1, 8, LANES), lambda j, *_: (j, 0, 0))
    delta, kept = session_call(
        functools.partial(delta_kernel, **sizes),
        scalars,
        slot_count,
        [x_op, b_op, steps_op, a_op, bias_op],
        [
            (shape(state_shape, f32), piece_block, by_slot),
            (shape((slot_count, 8, LANES), f32), *kept_block),
        ],
        4_000_000_000,
        "delta_states",
    )

    (closing,) = session_call(
        functools.partial(closing_kernel, heads=heads),
        (),
        slot_count,
        [(start, piece_block, by_slot), (delta, piece_block, by_slot), (kept, *kept_block)],
        [(shape(state_shape, bf16), piece_block, by_slot)],
        1_000_000_000,
        "closing_states",
    )
    closing, start = lax.optimization_barrier((closing, start))
    back = exchange(closing, req_size).reshape(req_size * slot_count, per, STATE)
    back = reorder(back, table, True)

    start_op = (start, piece_block, by_slot)
    (mixed,) = session_call(
        functools.partial(outputs_kernel, **sizes),
        scalars,
        slot_count,
        [x_op, b_op, c_op, steps_op, start_op, a_op, bias_op, skip_op],
        [(shape((total_rows, width), bf16), (MAXLEN, width), by_session)],
        10_000_000_000,
        "session_outputs",
    )
    sent = local_call(
        split_kernel,
        place,
        (mixed.reshape(tensor_size, rows, width),),
        [shape((GROUPS, rows, width), bf16)] * side,
        "split_rows",
    )
    sent = local_call(
        turn_out_kernel,
        place,
        send_along(sent, side, False),
        [shape((rows, side * width), bf16)] * GROUPS,
        "turn_out",
    )
    back, *sent = lax.optimization_barrier((back, *sent))
    back = exchange(back.reshape(state_shape), req_size)
    new_cache = back.transpose(1, 0, 2, 3).reshape(state_cache.shape)
    y_out = local_call(
        columns_kernel,
        place,
        send_along(sent, side, True),
        shape(x_in.shape, bf16),
        "join_columns",
    )
    return y_out, new_cache


def solution(mesh):
    tokens = P(("req", "tensor"), None)
    states = P("req", "tensor", None, None)
    placed = (tokens,) * 4 + (P("tensor"),) * 3 + (states,) + (P(),) * 4
    return jax.shard_map(
        per_device,
        mesh=mesh,
        in_specs=placed,
        out_specs=(tokens, states),
        check_vma=False,
    )
```

```python
import functools

import jax
import jax.numpy as jnp
from jax import lax
from jax.experimental import pallas as pl
from jax.experimental.pallas import tpu as pltpu
from jax.sharding import PartitionSpec as P

HEADS = 128
HEAD_DIM = 64
STATE = 128
GROUPS = 4
MAXLEN = 192
LANES = 128
VMEM_LIMIT = 20 * 1024 * 1024


def pack_kernel(place_ref, x_ref, dt_ref, b_ref, c_ref, *out_refs):
    parts = len(out_refs)
    width = x_ref.shape[1] // parts
    for shift, out_ref in enumerate(out_refs):
        target = lax.rem(place_ref[2] + shift, parts)
        group = pl.ds(pl.multiple_of(target * STATE, LANES), STATE)
        out_ref[:, :width] = x_ref[:, pl.ds(pl.multiple_of(target * width, LANES), width)]
        out_ref[:, width : width + STATE] = b_ref[:, group]
        out_ref[:, width + STATE : width + 2 * STATE] = c_ref[:, group]
        out_ref[:, width + 2 * STATE :] = dt_ref[...]


def turn_in_kernel(place_ref, *refs):
    half = len(refs) // 2
    extra = 2 * STATE + HEADS
    width = (refs[0].shape[1] - extra) // half
    for shift in range(half):
        target = lax.rem(place_ref[3] + shift, half)
        columns = pl.ds(pl.multiple_of(target * width, LANES), width)
        for row in range(half):
            refs[half + shift][row, :, :width] = refs[row][:, columns]
            refs[half + shift][row, :, width:] = refs[row][:, half * width :]


def gather_kernel(place_ref, *refs):
    out_ref = refs[-1]
    parts = len(refs) - 1
    for across in range(parts):
        x_from = lax.rem(place_ref[3] + parts - across, parts)
        for down in range(parts):
            y_from = lax.rem(place_ref[2] + parts - down, parts)
            out_ref[y_from * parts + x_from] = refs[across][down]


def split_kernel(place_ref, rows_ref, *out_refs):
    parts = len(out_refs)
    for across, out_ref in enumerate(out_refs):
        x_to = lax.rem(place_ref[3] + across, parts)
        for down in range(parts):
            y_to = lax.rem(place_ref[2] + down, parts)
            out_ref[down] = rows_ref[y_to * parts + x_to]


def turn_out_kernel(place_ref, *refs):
    half = len(refs) // 2
    width = refs[0].shape[2]
    for across in range(half):
        x_from = lax.rem(place_ref[3] + half - across, half)
        columns = pl.ds(pl.multiple_of(x_from * width, LANES), width)
        for down in range(half):
            refs[half + down][:, columns] = refs[across][down]


def columns_kernel(place_ref, *refs):
    out_ref = refs[-1]
    parts = len(refs) - 1
    width = refs[0].shape[1]
    for shift in range(parts):
        source = lax.rem(place_ref[2] + parts - shift, parts)
        out_ref[:, pl.ds(pl.multiple_of(source * width, LANES), width)] = refs[shift][...]


def local_call(kernel, place, arrays, out_shape, name):
    smem = pl.BlockSpec(memory_space=pltpu.SMEM)
    vmem = pl.BlockSpec(memory_space=pltpu.VMEM)
    several = isinstance(out_shape, list)
    return pl.pallas_call(
        kernel,
        in_specs=[smem] + [vmem] * len(arrays),
        out_specs=[vmem] * len(out_shape) if several else vmem,
        out_shape=out_shape,
        compiler_params=pltpu.CompilerParams(vmem_limit_bytes=VMEM_LIMIT),
        name=name,
    )(place, *arrays)


def moved_by(count, down, across):
    return [
        (i, (i // count + down) % count * count + (i % count + across) % count)
        for i in range(count * count)
    ]


def send_along(arrays, count, along_y):
    moved = list(arrays)
    for shift in sorted(range(1, count), key=lambda d: -min(d, count - d)):
        pairs = moved_by(count, shift, 0) if along_y else moved_by(count, 0, shift)
        moved[shift] = lax.ppermute(arrays[shift], "tensor", pairs)
    return moved


def member_at(spot, count):
    chips = count // 2
    return lax.rem(lax.rem(spot, chips) * 3, chips) * 2 + spot // chips


def spot_of(member, count):
    chips = count // 2
    return lax.rem(member, 2) * chips + lax.rem(member // 2 * 11, chips)


def members(count):
    chips = count // 2
    return [spot % chips * 3 % chips * 2 + spot // chips for spot in range(count)]


def rows_kernel(sessions_ref, owners_ref, slots_ref, rows_ref, *, slot_count):
    count = rows_ref.shape[0] // slot_count

    def step(spot, carry):
        group = member_at(spot, count)
        for slot in range(slot_count):
            session = sessions_ref[group * slot_count + slot]
            owner = spot_of(owners_ref[session], count)
            rows_ref[spot * slot_count + slot] = owner * slot_count + slots_ref[session]
        return carry

    lax.fori_loop(0, count, step, 0)


def cache_rows(sessions, owners, slots, slot_count):
    smem = pl.BlockSpec(memory_space=pltpu.SMEM)
    return pl.pallas_call(
        functools.partial(rows_kernel, slot_count=slot_count),
        in_specs=[smem] * 3,
        out_specs=smem,
        out_shape=jax.ShapeDtypeStruct(sessions.shape, jnp.int32),
        name="cache_rows",
    )(sessions, owners, slots)


def order_kernel(rows_ref, in_ref, out_ref, *, to_owner):
    def step(index, carry):
        row = rows_ref[index]
        if to_owner:
            out_ref[row] = in_ref[index]
        else:
            out_ref[index] = in_ref[row]
        return carry

    lax.fori_loop(0, in_ref.shape[0], step, 0, unroll=16)


def reorder(pieces, rows, to_owner):
    smem = pl.BlockSpec(memory_space=pltpu.SMEM)
    vmem = pl.BlockSpec(memory_space=pltpu.VMEM)
    return pl.pallas_call(
        functools.partial(order_kernel, to_owner=to_owner),
        in_specs=[smem, vmem],
        out_specs=vmem,
        out_shape=jax.ShapeDtypeStruct(pieces.shape, pieces.dtype),
        compiler_params=pltpu.CompilerParams(vmem_limit_bytes=VMEM_LIMIT),
        name="to_owner_order" if to_owner else "to_group_order",
    )(rows, pieces)


def exchange(states, axis_size, split_axis=0):
    return lax.all_to_all(
        states, "req", split_axis=split_axis, concat_axis=0, axis_index_groups=[members(axis_size)]
    )


def token_steps(place_ref, steps_ref, bias_ref, a_log_ref, length, heads):
    f32 = jnp.float32
    lane_from = lax.broadcasted_iota(jnp.int32, (HEADS, LANES), 0)
    lane_to = lax.broadcasted_iota(jnp.int32, (HEADS, LANES), 1)
    chosen = (lane_from == lane_to + place_ref[1] * heads) & (lane_to < heads)
    raw = jnp.dot(steps_ref[...], chosen.astype(jnp.bfloat16), preferred_element_type=f32)
    row_index = lax.broadcasted_iota(jnp.int32, (MAXLEN, LANES), 0)
    shifted = raw + bias_ref[...]
    soft = jnp.maximum(shifted, 0.0) + jnp.log(1.0 + jnp.exp(-jnp.abs(shifted)))
    live = row_index < length
    step = jnp.where(live, soft, 0.0)
    t_index = lax.broadcasted_iota(jnp.int32, (MAXLEN, MAXLEN), 0)
    u_index = lax.broadcasted_iota(jnp.int32, (MAXLEN, MAXLEN), 1)
    causal = t_index >= u_index
    cum = jnp.dot(
        causal.astype(f32),
        step * -jnp.exp(a_log_ref[...]),
        precision=lax.Precision.HIGHEST,
        preferred_element_type=f32,
    )
    return step, cum, live, causal


def spread(columns, first, left):
    one = jnp.broadcast_to(columns[:, first : first + 1], left.shape)
    two = jnp.broadcast_to(columns[:, first + 1 : first + 2], left.shape)
    return jnp.where(left, one, two)


def left_half():
    return lax.broadcasted_iota(jnp.int32, (MAXLEN, LANES), 1) < HEAD_DIM


def delta_kernel(
    place_ref, sessions_ref, lengths_ref, x_ref, b_ref, steps_ref, a_log_ref, bias_ref,
    delta_ref, kept_ref, *, heads, slot_count
):
    length = lengths_ref[sessions_ref[place_ref[0] * slot_count + pl.program_id(0)]]
    step, cum, _, _ = token_steps(place_ref, steps_ref, bias_ref, a_log_ref, length, heads)
    last = cum[MAXLEN - 1 : MAXLEN, :]
    to_end = jnp.exp(last - cum) * step
    kept_ref[0] = jnp.broadcast_to(jnp.exp(last), kept_ref.shape[1:])
    left = left_half()
    in_proj = b_ref[...]
    per = delta_ref.shape[2]
    for first in range(0, heads, 2):
        lanes = slice(first * HEAD_DIM, (first + 2) * HEAD_DIM)
        scaled = x_ref[:, lanes].astype(jnp.float32) * spread(to_end, first, left)
        added = lax.dot_general(
            scaled.astype(jnp.bfloat16),
            in_proj,
            (((0,), (0,)), ((), ())),
            preferred_element_type=jnp.float32,
        )
        begin, count = first * HEAD_DIM // per, 2 * HEAD_DIM // per
        delta_ref[begin : begin + count, 0] = added.reshape(count, per, STATE)


def closing_kernel(start_ref, delta_ref, kept_ref, closing_ref, *, heads):
    per = start_ref.shape[2]
    count = HEAD_DIM // per
    for head in range(heads):
        rows = slice(head * count, (head + 1) * count)
        kept = kept_ref[0, :1, head : head + 1].reshape(1, 1, 1)
        closing = kept * start_ref[rows, 0].astype(jnp.float32) + delta_ref[rows, 0]
        closing_ref[rows, 0] = closing.astype(jnp.bfloat16)


def outputs_kernel(
    place_ref, sessions_ref, lengths_ref, x_ref, b_ref, c_ref, steps_ref, start_ref, a_log_ref,
    bias_ref, skip_ref, y_ref, *, heads, slot_count
):
    f32 = jnp.float32
    bf16 = jnp.bfloat16
    half = LANES
    width = heads * HEAD_DIM
    length = lengths_ref[sessions_ref[place_ref[0] * slot_count + pl.program_id(0)]]
    step, cum, live, causal = token_steps(
        place_ref, steps_ref, bias_ref, a_log_ref, length, heads
    )
    drop_rows = (cum - jnp.log(step)).T
    grown = jnp.exp(cum)
    out_proj = c_ref[...]
    affinity = lax.dot_general(
        out_proj, b_ref[...], (((1,), (1,)), ((), ())), preferred_element_type=f32
    )
    affinity = jnp.where(causal, affinity, 0.0)
    top, low = affinity[:half, :half], affinity[half:, :]
    carried = lax.dot_general(
        out_proj,
        start_ref[...].reshape(width, STATE),
        (((1,), (1,)), ((), ())),
        preferred_element_type=f32,
    )
    left = left_half()
    for first in range(0, heads, 2):
        lanes = slice(first * HEAD_DIM, (first + 2) * HEAD_DIM)
        pair = x_ref[:, lanes]
        mixed = []
        for head in (first, first + 1):
            column = cum[:, head : head + 1]
            line = drop_rows[head : head + 1, :]
            w_top = top * jnp.exp(jnp.minimum(column[:half] - line[:, :half], 80.0))
            w_low = low * jnp.exp(jnp.minimum(column[half:] - line, 80.0))
            mixed.append(
                jnp.concatenate(
                    [
                        jnp.dot(w_top.astype(bf16), pair[:half], preferred_element_type=f32),
                        jnp.dot(w_low.astype(bf16), pair, preferred_element_type=f32),
                    ],
                    axis=0,
                )
            )
        out = (
            jnp.where(left, mixed[0], mixed[1])
            + spread(grown, first, left) * carried[:, lanes]
            + skip_ref[:, lanes] * pair.astype(f32)
        )
        y_ref[:, lanes] = jnp.where(live, out, 0.0).astype(bf16)


def session_call(kernel, scalars, slot_count, operands, outputs, flops, name):
    return pl.pallas_call(
        kernel,
        grid_spec=pltpu.PrefetchScalarGridSpec(
            num_scalar_prefetch=len(scalars),
            grid=(slot_count,),
            in_specs=[pl.BlockSpec(block, index) for _, block, index in operands],
            out_specs=[pl.BlockSpec(block, index) for _, block, index in outputs],
        ),
        out_shape=[shape for shape, _, _ in outputs],
        compiler_params=pltpu.CompilerParams(vmem_limit_bytes=VMEM_LIMIT),
        cost_estimate=pl.CostEstimate(
            flops=flops, bytes_accessed=8 * 1024 * 1024, transcendentals=0
        ),
        name=name,
    )(*scalars, *(array for array, _, _ in operands))


def per_device(
    x_in,
    dt_raw,
    b_in,
    c_in,
    a_log,
    dt_bias,
    d_skip,
    state_cache,
    group_sessions,
    owners,
    cache_slots,
    lengths,
):
    tensor_size = lax.axis_size("tensor")
    req_size = lax.axis_size("req")
    slot_count, heads = state_cache.shape[:2]
    per = heads * HEAD_DIM // req_size
    side = tensor_size // GROUPS
    rows = x_in.shape[0]
    width = heads * HEAD_DIM
    bf16 = jnp.bfloat16
    f32 = jnp.float32
    shape = jax.ShapeDtypeStruct
    req_index = lax.axis_index("req")
    tensor_index = lax.axis_index("tensor")
    place = jnp.stack(
        [req_index, tensor_index, tensor_index // side, tensor_index % side]
    ).astype(jnp.int32)
    sessions = group_sessions.reshape(-1)

    state_shape = (req_size, slot_count, per, STATE)
    table = cache_rows(sessions, owners, cache_slots, slot_count)
    pieces = state_cache.reshape(slot_count, req_size, per, STATE)
    held = exchange(pieces, req_size, 1).reshape(req_size * slot_count, per, STATE)
    held = reorder(held, table, False)

    extra = 2 * STATE + HEADS
    sent = local_call(
        pack_kernel,
        place,
        (x_in, dt_raw, b_in, c_in),
        [shape((rows, side * width + extra), bf16)] * GROUPS,
        "pack_tokens",
    )
    sent = local_call(
        turn_in_kernel,
        place,
        send_along(sent, side, True),
        [shape((GROUPS, rows, width + extra), bf16)] * side,
        "turn_in",
    )
    sent = send_along(sent, side, False)
    held, sent[1] = lax.optimization_barrier((held, sent[1]))
    start = exchange(held.reshape(state_shape), req_size)
    packed = local_call(
        gather_kernel,
        place,
        sent,
        shape((tensor_size, rows, width + extra), bf16),
        "gather_tokens",
    ).reshape(tensor_size * rows, width + extra)

    pad = ((0, 0), (0, LANES - heads))
    a_row = jnp.pad(a_log[None, :], pad)
    bias_row = jnp.pad(dt_bias[None, :], pad)
    skip_row = jnp.repeat(d_skip, HEAD_DIM)[None, :]
    one_row = lambda j, *_: (0, 0)
    by_session = lambda j, *_: (j, 0)
    x_op = (packed, (MAXLEN, width), by_session)
    b_op = (packed, (MAXLEN, STATE), lambda j, *_: (j, width // STATE))
    c_op = (packed, (MAXLEN, STATE), lambda j, *_: (j, width // STATE + 1))
    steps_op = (packed, (MAXLEN, HEADS), lambda j, *_: (j, width // STATE + 2))
    a_op = (a_row, (1, LANES), one_row)
    bias_op = (bias_row, (1, LANES), one_row)
    skip_op = (skip_row, (1, width), one_row)
    scalars = (place, sessions, lengths)
    sizes = dict(heads=heads, slot_count=slot_count)
    piece_block = (req_size, 1, per, STATE)
    by_slot = lambda j, *_: (0, j, 0, 0)
    total_rows = tensor_size * rows

    kept_block = ((1, 8, LANES), lambda j, *_: (j, 0, 0))
    delta, kept = session_call(
        functools.partial(delta_kernel, **sizes),
        scalars,
        slot_count,
        [x_op, b_op, steps_op, a_op, bias_op],
        [
            (pltpu.HBM(state_shape, f32), piece_block, by_slot),
            (shape((slot_count, 8, LANES), f32), *kept_block),
        ],
        4_000_000_000,
        "delta_states",
    )

    (closing,) = session_call(
        functools.partial(closing_kernel, heads=heads),
        (),
        slot_count,
        [(start, piece_block, by_slot), (delta, piece_block, by_slot), (kept, *kept_block)],
        [(pltpu.HBM(state_shape, bf16), piece_block, by_slot)],
        1_000_000_000,
        "closing_states",
    )
    closing, start = lax.optimization_barrier((closing, start))
    back = exchange(closing, req_size).reshape(req_size * slot_count, per, STATE)
    back = reorder(back, table, True)

    start_op = (start, piece_block, by_slot)
    (mixed,) = session_call(
        functools.partial(outputs_kernel, **sizes),
        scalars,
        slot_count,
        [x_op, b_op, c_op, steps_op, start_op, a_op, bias_op, skip_op],
        [(shape((total_rows, width), bf16), (MAXLEN, width), by_session)],
        10_000_000_000,
        "session_outputs",
    )
    sent = local_call(
        split_kernel,
        place,
        (mixed.reshape(tensor_size, rows, width),),
        [shape((GROUPS, rows, width), bf16)] * side,
        "split_rows",
    )
    sent = local_call(
        turn_out_kernel,
        place,
        send_along(sent, side, False),
        [shape((rows, side * width), bf16)] * GROUPS,
        "turn_out",
    )
    back, *sent = lax.optimization_barrier((back, *sent))
    back = exchange(back.reshape(state_shape), req_size)
    new_cache = back.transpose(1, 0, 2, 3).reshape(state_cache.shape)
    y_out = local_call(
        columns_kernel,
        place,
        send_along(sent, side, True),
        shape(x_in.shape, bf16),
        "join_columns",
    )
    return y_out, new_cache


def solution(mesh):
    tokens = P(("req", "tensor"), None)
    states = P("req", "tensor", None, None)
    placed = (tokens,) * 4 + (P("tensor"),) * 3 + (states,) + (P(),) * 4
    return jax.shard_map(
        per_device,
        mesh=mesh,
        in_specs=placed,
        out_specs=(tokens, states),
        check_vma=False,
    )
```

```python
import functools

import jax
import jax.numpy as jnp
from jax import lax
from jax.experimental import pallas as pl
from jax.experimental.pallas import tpu as pltpu
from jax.sharding import PartitionSpec as P

HEADS = 128
HEAD_DIM = 64
STATE = 128
GROUPS = 4
MAXLEN = 192
LANES = 128
VMEM_LIMIT = 20 * 1024 * 1024


def pack_kernel(place_ref, x_ref, dt_ref, b_ref, c_ref, *out_refs):
    parts = len(out_refs)
    width = x_ref.shape[1] // parts
    for shift, out_ref in enumerate(out_refs):
        target = lax.rem(place_ref[2] + shift, parts)
        group = pl.ds(pl.multiple_of(target * STATE, LANES), STATE)
        out_ref[:, :width] = x_ref[:, pl.ds(pl.multiple_of(target * width, LANES), width)]
        out_ref[:, width : width + STATE] = b_ref[:, group]
        out_ref[:, width + STATE : width + 2 * STATE] = c_ref[:, group]
        out_ref[:, width + 2 * STATE :] = dt_ref[...]


def long_first(count):
    return sorted(range(count), key=lambda d: (d != 0, -min(d, count - d)))


def turn_in_kernel(place_ref, *refs):
    half = len(refs) // 2
    extra = 2 * STATE + HEADS
    width = (refs[0].shape[1] - extra) // half
    for shift in range(half):
        target = lax.rem(place_ref[3] + shift, half)
        columns = pl.ds(pl.multiple_of(target * width, LANES), width)
        for place, row in enumerate(long_first(half)):
            refs[half + shift][row, :, :width] = refs[place][:, columns]
            refs[half + shift][row, :, width:] = refs[place][:, half * width :]


def gather_kernel(place_ref, *refs):
    out_ref = refs[-1]
    parts = len(refs) - 1
    for across in range(parts):
        x_from = lax.rem(place_ref[3] + parts - across, parts)
        for down in range(parts):
            y_from = lax.rem(place_ref[2] + parts - down, parts)
            out_ref[y_from * parts + x_from] = refs[across][down]


def split_kernel(place_ref, rows_ref, *out_refs):
    parts = len(out_refs)
    for across, out_ref in enumerate(out_refs):
        x_to = lax.rem(place_ref[3] + across, parts)
        for down in range(parts):
            y_to = lax.rem(place_ref[2] + down, parts)
            out_ref[down] = rows_ref[y_to * parts + x_to]


def turn_out_kernel(place_ref, *refs):
    half = len(refs) // 2
    width = refs[0].shape[2]
    for across in range(half):
        x_from = lax.rem(place_ref[3] + half - across, half)
        columns = pl.ds(pl.multiple_of(x_from * width, LANES), width)
        for down in range(half):
            refs[half + down][:, columns] = refs[across][down]


def columns_kernel(place_ref, *refs):
    out_ref = refs[-1]
    parts = len(refs) - 1
    width = refs[0].shape[1]
    for shift in range(parts):
        source = lax.rem(place_ref[2] + parts - shift, parts)
        out_ref[:, pl.ds(pl.multiple_of(source * width, LANES), width)] = refs[shift][...]


def local_call(kernel, place, arrays, out_shape, name):
    smem = pl.BlockSpec(memory_space=pltpu.SMEM)
    vmem = pl.BlockSpec(memory_space=pltpu.VMEM)
    several = isinstance(out_shape, list)
    return pl.pallas_call(
        kernel,
        in_specs=[smem] + [vmem] * len(arrays),
        out_specs=[vmem] * len(out_shape) if several else vmem,
        out_shape=out_shape,
        compiler_params=pltpu.CompilerParams(vmem_limit_bytes=VMEM_LIMIT),
        name=name,
    )(place, *arrays)


def moved_by(count, down, across):
    return [
        (i, (i // count + down) % count * count + (i % count + across) % count)
        for i in range(count * count)
    ]


def send_along(arrays, count, along_y):
    moved = list(arrays)
    for shift in long_first(count)[1:]:
        pairs = moved_by(count, shift, 0) if along_y else moved_by(count, 0, shift)
        moved[shift] = lax.ppermute(arrays[shift], "tensor", pairs)
    return moved


def member_at(spot, count):
    chips = count // 2
    core = lax.rem(spot, 2)
    return lax.rem(spot // 2 * 7 + core * (chips // 2), chips) * 2 + core


def spot_of(member, count):
    chips = count // 2
    core = lax.rem(member, 2)
    return lax.rem((member // 2 + core * (chips // 2)) * 7, chips) * 2 + core


def members(count):
    chips = count // 2
    return [(spot // 2 * 7 + spot % 2 * (chips // 2)) % chips * 2 + spot % 2 for spot in range(count)]


def rows_kernel(sessions_ref, owners_ref, slots_ref, rows_ref, *, slot_count):
    count = rows_ref.shape[0] // slot_count

    def step(spot, carry):
        group = member_at(spot, count)
        for slot in range(slot_count):
            session = sessions_ref[group * slot_count + slot]
            owner = spot_of(owners_ref[session], count)
            rows_ref[spot * slot_count + slot] = owner * slot_count + slots_ref[session]
        return carry

    lax.fori_loop(0, count, step, 0)


def cache_rows(sessions, owners, slots, slot_count):
    smem = pl.BlockSpec(memory_space=pltpu.SMEM)
    return pl.pallas_call(
        functools.partial(rows_kernel, slot_count=slot_count),
        in_specs=[smem] * 3,
        out_specs=smem,
        out_shape=jax.ShapeDtypeStruct(sessions.shape, jnp.int32),
        name="cache_rows",
    )(sessions, owners, slots)


def order_kernel(rows_ref, in_ref, out_ref, *, to_owner):
    def step(index, carry):
        row = rows_ref[index]
        if to_owner:
            out_ref[row] = in_ref[index]
        else:
            out_ref[index] = in_ref[row]
        return carry

    lax.fori_loop(0, in_ref.shape[0], step, 0, unroll=16)


def reorder(pieces, rows, to_owner):
    smem = pl.BlockSpec(memory_space=pltpu.SMEM)
    vmem = pl.BlockSpec(memory_space=pltpu.VMEM)
    return pl.pallas_call(
        functools.partial(order_kernel, to_owner=to_owner),
        in_specs=[smem, vmem],
        out_specs=vmem,
        out_shape=jax.ShapeDtypeStruct(pieces.shape, pieces.dtype),
        compiler_params=pltpu.CompilerParams(vmem_limit_bytes=VMEM_LIMIT),
        name="to_owner_order" if to_owner else "to_group_order",
    )(rows, pieces)


def exchange(states, axis_size, split_axis=0):
    return lax.all_to_all(
        states, "req", split_axis=split_axis, concat_axis=0, axis_index_groups=[members(axis_size)]
    )


def steps_kernel(
    place_ref, sessions_ref, lengths_ref, raw_ref, bias_ref, a_log_ref, step_ref, cum_ref, *, heads
):
    f32 = jnp.float32
    slot_count = step_ref.shape[0]
    lane_from = lax.broadcasted_iota(jnp.int32, (HEADS, LANES), 0)
    lane_to = lax.broadcasted_iota(jnp.int32, (HEADS, LANES), 1)
    row_index = lax.broadcasted_iota(jnp.int32, (MAXLEN, LANES), 0)
    lane_index = lax.broadcasted_iota(jnp.int32, (MAXLEN, LANES), 1)
    raw = jnp.zeros((MAXLEN, LANES), f32)
    length = jnp.zeros((MAXLEN, LANES), jnp.int32)
    for slot in range(slot_count):
        head = lane_to - slot * heads
        chosen = (lane_from == head + place_ref[1] * heads) & (head >= 0) & (head < heads)
        raw += jnp.dot(
            raw_ref[slot * MAXLEN : (slot + 1) * MAXLEN, :],
            chosen.astype(jnp.bfloat16),
            preferred_element_type=f32,
        )
        session = sessions_ref[place_ref[0] * slot_count + slot]
        mine = (lane_index >= slot * heads) & (lane_index < (slot + 1) * heads)
        length = jnp.where(mine, lengths_ref[session], length)
    shifted = raw + bias_ref[...]
    soft = jnp.maximum(shifted, 0.0) + jnp.log(1.0 + jnp.exp(-jnp.abs(shifted)))
    step = jnp.where(row_index < length, soft, 0.0)
    t_index = lax.broadcasted_iota(jnp.int32, (MAXLEN, MAXLEN), 0)
    u_index = lax.broadcasted_iota(jnp.int32, (MAXLEN, MAXLEN), 1)
    cum = jnp.dot(
        (t_index >= u_index).astype(f32),
        step * -jnp.exp(a_log_ref[...]),
        precision=lax.Precision.HIGHEST,
        preferred_element_type=f32,
    )
    for slot in range(slot_count):
        back = (LANES - slot * heads) % LANES
        step_ref[slot] = pltpu.roll(step, back, 1) if back else step
        cum_ref[slot] = pltpu.roll(cum, back, 1) if back else cum


def spread(columns, first, left):
    one = jnp.broadcast_to(columns[:, first : first + 1], left.shape)
    two = jnp.broadcast_to(columns[:, first + 1 : first + 2], left.shape)
    return jnp.where(left, one, two)


def left_half():
    return lax.broadcasted_iota(jnp.int32, (MAXLEN, LANES), 1) < HEAD_DIM


def delta_kernel(
    x_ref, b_ref, step_ref, cum_ref, delta_ref, kept_ref, *, heads
):
    step, cum = step_ref[0], cum_ref[0]
    last = cum[MAXLEN - 1 : MAXLEN, :]
    to_end = jnp.exp(last - cum) * step
    kept_ref[0] = jnp.broadcast_to(jnp.exp(last), kept_ref.shape[1:])
    left = left_half()
    in_proj = b_ref[...]
    per = delta_ref.shape[2]
    for first in range(0, heads, 2):
        lanes = slice(first * HEAD_DIM, (first + 2) * HEAD_DIM)
        scaled = x_ref[:, lanes].astype(jnp.float32) * spread(to_end, first, left)
        added = lax.dot_general(
            scaled.astype(jnp.bfloat16),
            in_proj,
            (((0,), (0,)), ((), ())),
            preferred_element_type=jnp.float32,
        )
        begin, count = first * HEAD_DIM // per, 2 * HEAD_DIM // per
        delta_ref[begin : begin + count, 0] = added.reshape(count, per, STATE)


def closing_kernel(start_ref, delta_ref, kept_ref, closing_ref, *, heads):
    per = start_ref.shape[2]
    count = HEAD_DIM // per
    for head in range(heads):
        rows = slice(head * count, (head + 1) * count)
        kept = kept_ref[0, :1, head : head + 1].reshape(1, 1, 1)
        closing = kept * start_ref[rows, 0].astype(jnp.float32) + delta_ref[rows, 0]
        closing_ref[rows, 0] = closing.astype(jnp.bfloat16)


def outputs_kernel(
    place_ref, sessions_ref, lengths_ref, x_ref, b_ref, c_ref, step_ref, cum_ref, start_ref,
    skip_ref, y_ref, *, heads, slot_count
):
    f32 = jnp.float32
    bf16 = jnp.bfloat16
    half = LANES
    width = heads * HEAD_DIM
    length = lengths_ref[sessions_ref[place_ref[0] * slot_count + pl.program_id(0)]]
    step, cum = step_ref[0], cum_ref[0]
    live = lax.broadcasted_iota(jnp.int32, (MAXLEN, LANES), 0) < length
    t_index = lax.broadcasted_iota(jnp.int32, (MAXLEN, MAXLEN), 0)
    u_index = lax.broadcasted_iota(jnp.int32, (MAXLEN, MAXLEN), 1)
    causal = t_index >= u_index
    drop_rows = (cum - jnp.log(step)).T
    grown = jnp.exp(cum)
    out_proj = c_ref[...]
    affinity = lax.dot_general(
        out_proj, b_ref[...], (((1,), (1,)), ((), ())), preferred_element_type=f32
    )
    affinity = jnp.where(causal, affinity, 0.0)
    top, low = affinity[:half, :half], affinity[half:, :]
    carried = lax.dot_general(
        out_proj,
        start_ref[...].reshape(width, STATE),
        (((1,), (1,)), ((), ())),
        preferred_element_type=f32,
    )
    left = left_half()
    for first in range(0, heads, 2):
        lanes = slice(first * HEAD_DIM, (first + 2) * HEAD_DIM)
        pair = x_ref[:, lanes]
        mixed = []
        for head in (first, first + 1):
            column = cum[:, head : head + 1]
            line = drop_rows[head : head + 1, :]
            w_top = top * jnp.exp(jnp.minimum(column[:half] - line[:, :half], 80.0))
            w_low = low * jnp.exp(jnp.minimum(column[half:] - line, 80.0))
            mixed.append(
                jnp.concatenate(
                    [
                        jnp.dot(w_top.astype(bf16), pair[:half], preferred_element_type=f32),
                        jnp.dot(w_low.astype(bf16), pair, preferred_element_type=f32),
                    ],
                    axis=0,
                )
            )
        out = (
            jnp.where(left, mixed[0], mixed[1])
            + spread(grown, first, left) * carried[:, lanes]
            + skip_ref[:, lanes] * pair.astype(f32)
        )
        y_ref[:, lanes] = jnp.where(live, out, 0.0).astype(bf16)


def session_call(kernel, scalars, slot_count, operands, outputs, flops, name):
    return pl.pallas_call(
        kernel,
        grid_spec=pltpu.PrefetchScalarGridSpec(
            num_scalar_prefetch=len(scalars),
            grid=(slot_count,),
            in_specs=[pl.BlockSpec(block, index) for _, block, index in operands],
            out_specs=[pl.BlockSpec(block, index) for _, block, index in outputs],
        ),
        out_shape=[shape for shape, _, _ in outputs],
        compiler_params=pltpu.CompilerParams(vmem_limit_bytes=VMEM_LIMIT),
        cost_estimate=pl.CostEstimate(
            flops=flops, bytes_accessed=8 * 1024 * 1024, transcendentals=0
        ),
        name=name,
    )(*scalars, *(array for array, _, _ in operands))


def per_device(
    x_in,
    dt_raw,
    b_in,
    c_in,
    a_log,
    dt_bias,
    d_skip,
    state_cache,
    group_sessions,
    owners,
    cache_slots,
    lengths,
):
    tensor_size = lax.axis_size("tensor")
    req_size = lax.axis_size("req")
    slot_count, heads = state_cache.shape[:2]
    per = heads * HEAD_DIM // req_size
    side = tensor_size // GROUPS
    rows = x_in.shape[0]
    width = heads * HEAD_DIM
    bf16 = jnp.bfloat16
    f32 = jnp.float32
    shape = jax.ShapeDtypeStruct
    req_index = lax.axis_index("req")
    tensor_index = lax.axis_index("tensor")
    place = jnp.stack(
        [req_index, tensor_index, tensor_index // side, tensor_index % side]
    ).astype(jnp.int32)
    sessions = group_sessions.reshape(-1)

    state_shape = (req_size, slot_count, per, STATE)
    table = cache_rows(sessions, owners, cache_slots, slot_count)
    pieces = state_cache.reshape(slot_count, req_size, per, STATE)
    held = exchange(pieces, req_size, 1).reshape(req_size * slot_count, per, STATE)
    held = reorder(held, table, False)

    extra = 2 * STATE + HEADS
    sent = local_call(
        pack_kernel,
        place,
        (x_in, dt_raw, b_in, c_in),
        [shape((rows, side * width + extra), bf16)] * GROUPS,
        "pack_tokens",
    )
    sent = local_call(
        turn_in_kernel,
        place,
        [send_along(sent, side, True)[shift] for shift in long_first(side)],
        [shape((GROUPS, rows, width + extra), bf16)] * side,
        "turn_in",
    )
    sent = send_along(sent, side, False)
    held, sent[1] = lax.optimization_barrier((held, sent[1]))
    start = exchange(held.reshape(state_shape), req_size)
    packed = local_call(
        gather_kernel,
        place,
        sent,
        shape((tensor_size, rows, width + extra), bf16),
        "gather_tokens",
    ).reshape(tensor_size * rows, width + extra)

    pad = ((0, 0), (0, LANES - slot_count * heads))
    a_row = jnp.pad(jnp.tile(a_log, slot_count)[None, :], pad)
    bias_row = jnp.pad(jnp.tile(dt_bias, slot_count)[None, :], pad)
    skip_row = jnp.repeat(d_skip, HEAD_DIM)[None, :]
    one_row = lambda j, *_: (0, 0)
    by_session = lambda j, *_: (j, 0)
    x_op = (packed, (MAXLEN, width), by_session)
    b_op = (packed, (MAXLEN, STATE), lambda j, *_: (j, width // STATE))
    c_op = (packed, (MAXLEN, STATE), lambda j, *_: (j, width // STATE + 1))
    skip_op = (skip_row, (1, width), one_row)
    scalars = (place, sessions, lengths)
    sizes = dict(heads=heads, slot_count=slot_count)
    piece_block = (req_size, 1, per, STATE)
    by_slot = lambda j, *_: (0, j, 0, 0)
    total_rows = tensor_size * rows

    kept_block = ((1, 8, LANES), lambda j, *_: (j, 0, 0))
    step, cum = pl.pallas_call(
        functools.partial(steps_kernel, heads=heads),
        grid_spec=pltpu.PrefetchScalarGridSpec(
            num_scalar_prefetch=len(scalars),
            grid=(1,),
            in_specs=[
                pl.BlockSpec((total_rows, HEADS), lambda j, *_: (0, width // HEADS + 2)),
                pl.BlockSpec((1, LANES), one_row),
                pl.BlockSpec((1, LANES), one_row),
            ],
            out_specs=[pl.BlockSpec((slot_count, MAXLEN, LANES), lambda j, *_: (0, 0, 0))] * 2,
        ),
        out_shape=[shape((slot_count, MAXLEN, LANES), f32)] * 2,
        compiler_params=pltpu.CompilerParams(vmem_limit_bytes=VMEM_LIMIT),
        name="steps",
    )(*scalars, packed, bias_row, a_row)
    step_block = ((1, MAXLEN, LANES), lambda j, *_: (j, 0, 0))
    step_op, cum_op = (step, *step_block), (cum, *step_block)

    delta, kept = session_call(
        functools.partial(delta_kernel, heads=heads),
        (),
        slot_count,
        [x_op, b_op, step_op, cum_op],
        [
            (pltpu.HBM(state_shape, f32), piece_block, by_slot),
            (shape((slot_count, 8, LANES), f32), *kept_block),
        ],
        4_000_000_000,
        "delta_states",
    )

    delta_held = pltpu.with_memory_space_constraint(delta, pltpu.HBM)
    (closing,) = session_call(
        functools.partial(closing_kernel, heads=heads),
        (),
        slot_count,
        [(start, piece_block, by_slot), (delta_held, piece_block, by_slot), (kept, *kept_block)],
        [(pltpu.HBM(state_shape, bf16), piece_block, by_slot)],
        1_000_000_000,
        "closing_states",
    )
    closing, start = lax.optimization_barrier((closing, start))
    back = exchange(closing, req_size).reshape(req_size * slot_count, per, STATE)
    back = reorder(back, table, True)

    start_op = (start, piece_block, by_slot)
    (mixed,) = session_call(
        functools.partial(outputs_kernel, **sizes),
        scalars,
        slot_count,
        [x_op, b_op, c_op, step_op, cum_op, start_op, skip_op],
        [(shape((total_rows, width), bf16), (MAXLEN, width), by_session)],
        10_000_000_000,
        "session_outputs",
    )
    sent = local_call(
        split_kernel,
        place,
        (mixed.reshape(tensor_size, rows, width),),
        [shape((GROUPS, rows, width), bf16)] * side,
        "split_rows",
    )
    sent = local_call(
        turn_out_kernel,
        place,
        send_along(sent, side, False),
        [shape((rows, side * width), bf16)] * GROUPS,
        "turn_out",
    )
    back, *sent = lax.optimization_barrier((back, *sent))
    back = exchange(back.reshape(state_shape), req_size)
    new_cache = back.transpose(1, 0, 2, 3).reshape(state_cache.shape)
    y_out = local_call(
        columns_kernel,
        place,
        send_along(sent, side, True),
        shape(x_in.shape, bf16),
        "join_columns",
    )
    return y_out, new_cache


def solution(mesh):
    tokens = P(("req", "tensor"), None)
    states = P("req", "tensor", None, None)
    placed = (tokens,) * 4 + (P("tensor"),) * 3 + (states,) + (P(),) * 4
    return jax.shard_map(
        per_device,
        mesh=mesh,
        in_specs=placed,
        out_specs=(tokens, states),
        check_vma=False,
    )
```

```python
import functools

import jax
import jax.numpy as jnp
from jax import lax
from jax.experimental import pallas as pl
from jax.experimental.pallas import tpu as pltpu
from jax.sharding import PartitionSpec as P

HEADS = 128
HEAD_DIM = 64
STATE = 128
GROUPS = 4
MAXLEN = 192
LANES = 128
VMEM_LIMIT = 20 * 1024 * 1024


def pack_kernel(place_ref, x_ref, dt_ref, b_ref, c_ref, *out_refs):
    parts = len(out_refs)
    width = x_ref.shape[1] // parts
    for shift, out_ref in enumerate(out_refs):
        target = lax.rem(place_ref[2] + shift, parts)
        group = pl.ds(pl.multiple_of(target * STATE, LANES), STATE)
        out_ref[:, :width] = x_ref[:, pl.ds(pl.multiple_of(target * width, LANES), width)]
        out_ref[:, width : width + STATE] = b_ref[:, group]
        out_ref[:, width + STATE : width + 2 * STATE] = c_ref[:, group]
        out_ref[:, width + 2 * STATE :] = dt_ref[...]


def long_first(count):
    return sorted(range(count), key=lambda d: (d != 0, -min(d, count - d)))


def turn_in_kernel(place_ref, *refs):
    half = len(refs) // 2
    extra = 2 * STATE + HEADS
    width = (refs[0].shape[1] - extra) // half
    for shift in range(half):
        target = lax.rem(place_ref[3] + shift, half)
        columns = pl.ds(pl.multiple_of(target * width, LANES), width)
        for place, row in enumerate(long_first(half)):
            refs[half + shift][row, :, :width] = refs[place][:, columns]
            refs[half + shift][row, :, width:] = refs[place][:, half * width :]


def gather_kernel(place_ref, *refs):
    out_ref = refs[-1]
    parts = len(refs) - 1
    for across in range(parts):
        x_from = lax.rem(place_ref[3] + parts - across, parts)
        for down in range(parts):
            y_from = lax.rem(place_ref[2] + parts - down, parts)
            out_ref[y_from * parts + x_from] = refs[across][down]


def split_kernel(place_ref, rows_ref, *out_refs):
    parts = len(out_refs)
    for across, out_ref in enumerate(out_refs):
        x_to = lax.rem(place_ref[3] + across, parts)
        for down in range(parts):
            y_to = lax.rem(place_ref[2] + down, parts)
            out_ref[down] = rows_ref[y_to * parts + x_to]


def turn_out_kernel(place_ref, *refs):
    half = len(refs) // 2
    width = refs[0].shape[2]
    for across in range(half):
        x_from = lax.rem(place_ref[3] + half - across, half)
        columns = pl.ds(pl.multiple_of(x_from * width, LANES), width)
        for down in range(half):
            refs[half + down][:, columns] = refs[across][down]


def columns_kernel(place_ref, *refs):
    out_ref = refs[-1]
    parts = len(refs) - 1
    width = refs[0].shape[1]
    for shift in range(parts):
        source = lax.rem(place_ref[2] + parts - shift, parts)
        out_ref[:, pl.ds(pl.multiple_of(source * width, LANES), width)] = refs[shift][...]


def local_call(kernel, place, arrays, out_shape, name):
    smem = pl.BlockSpec(memory_space=pltpu.SMEM)
    vmem = pl.BlockSpec(memory_space=pltpu.VMEM)
    several = isinstance(out_shape, list)
    return pl.pallas_call(
        kernel,
        in_specs=[smem] + [vmem] * len(arrays),
        out_specs=[vmem] * len(out_shape) if several else vmem,
        out_shape=out_shape,
        compiler_params=pltpu.CompilerParams(vmem_limit_bytes=VMEM_LIMIT),
        name=name,
    )(place, *arrays)


def moved_by(count, down, across):
    return [
        (i, (i // count + down) % count * count + (i % count + across) % count)
        for i in range(count * count)
    ]


def send_along(arrays, count, along_y):
    moved = list(arrays)
    for shift in long_first(count)[1:]:
        pairs = moved_by(count, shift, 0) if along_y else moved_by(count, 0, shift)
        moved[shift] = lax.ppermute(arrays[shift], "tensor", pairs)
    return moved


def member_at(spot, count):
    chips = count // 2
    return lax.rem(lax.rem(spot, chips) * 3, chips) * 2 + spot // chips


def spot_of(member, count):
    chips = count // 2
    return lax.rem(member, 2) * chips + lax.rem(member // 2 * 11, chips)


def members(count):
    chips = count // 2
    return [spot % chips * 3 % chips * 2 + spot // chips for spot in range(count)]


def rows_kernel(sessions_ref, owners_ref, slots_ref, rows_ref, *, slot_count):
    count = rows_ref.shape[0] // slot_count

    def step(spot, carry):
        group = member_at(spot, count)
        for slot in range(slot_count):
            session = sessions_ref[group * slot_count + slot]
            owner = spot_of(owners_ref[session], count)
            rows_ref[spot * slot_count + slot] = owner * slot_count + slots_ref[session]
        return carry

    lax.fori_loop(0, count, step, 0)


def cache_rows(sessions, owners, slots, slot_count):
    smem = pl.BlockSpec(memory_space=pltpu.SMEM)
    return pl.pallas_call(
        functools.partial(rows_kernel, slot_count=slot_count),
        in_specs=[smem] * 3,
        out_specs=smem,
        out_shape=jax.ShapeDtypeStruct(sessions.shape, jnp.int32),
        name="cache_rows",
    )(sessions, owners, slots)


def order_kernel(rows_ref, in_ref, out_ref, *, to_owner):
    def step(index, carry):
        row = rows_ref[index]
        if to_owner:
            out_ref[row] = in_ref[index]
        else:
            out_ref[index] = in_ref[row]
        return carry

    lax.fori_loop(0, in_ref.shape[0], step, 0, unroll=16)


def reorder(pieces, rows, to_owner):
    smem = pl.BlockSpec(memory_space=pltpu.SMEM)
    vmem = pl.BlockSpec(memory_space=pltpu.VMEM)
    return pl.pallas_call(
        functools.partial(order_kernel, to_owner=to_owner),
        in_specs=[smem, vmem],
        out_specs=vmem,
        out_shape=jax.ShapeDtypeStruct(pieces.shape, pieces.dtype),
        compiler_params=pltpu.CompilerParams(vmem_limit_bytes=VMEM_LIMIT),
        name="to_owner_order" if to_owner else "to_group_order",
    )(rows, pieces)


def exchange(states, axis_size, split_axis=0):
    return lax.all_to_all(
        states, "req", split_axis=split_axis, concat_axis=0, axis_index_groups=[members(axis_size)]
    )


def steps_kernel(
    place_ref, sessions_ref, lengths_ref, raw_ref, bias_ref, a_log_ref, step_ref, cum_ref, *, heads
):
    f32 = jnp.float32
    slot_count = step_ref.shape[0]
    lane_from = lax.broadcasted_iota(jnp.int32, (HEADS, LANES), 0)
    lane_to = lax.broadcasted_iota(jnp.int32, (HEADS, LANES), 1)
    row_index = lax.broadcasted_iota(jnp.int32, (MAXLEN, LANES), 0)
    lane_index = lax.broadcasted_iota(jnp.int32, (MAXLEN, LANES), 1)
    raw = jnp.zeros((MAXLEN, LANES), f32)
    length = jnp.zeros((MAXLEN, LANES), jnp.int32)
    for slot in range(slot_count):
        head = lane_to - slot * heads
        chosen = (lane_from == head + place_ref[1] * heads) & (head >= 0) & (head < heads)
        raw += jnp.dot(
            raw_ref[slot * MAXLEN : (slot + 1) * MAXLEN, :],
            chosen.astype(jnp.bfloat16),
            preferred_element_type=f32,
        )
        session = sessions_ref[place_ref[0] * slot_count + slot]
        mine = (lane_index >= slot * heads) & (lane_index < (slot + 1) * heads)
        length = jnp.where(mine, lengths_ref[session], length)
    shifted = raw + bias_ref[...]
    soft = jnp.maximum(shifted, 0.0) + jnp.log(1.0 + jnp.exp(-jnp.abs(shifted)))
    step = jnp.where(row_index < length, soft, 0.0)
    t_index = lax.broadcasted_iota(jnp.int32, (MAXLEN, MAXLEN), 0)
    u_index = lax.broadcasted_iota(jnp.int32, (MAXLEN, MAXLEN), 1)
    cum = jnp.dot(
        (t_index >= u_index).astype(f32),
        step * -jnp.exp(a_log_ref[...]),
        precision=lax.Precision.HIGHEST,
        preferred_element_type=f32,
    )
    for slot in range(slot_count):
        back = (LANES - slot * heads) % LANES
        step_ref[slot] = pltpu.roll(step, back, 1) if back else step
        cum_ref[slot] = pltpu.roll(cum, back, 1) if back else cum


def spread(columns, first, left):
    one = jnp.broadcast_to(columns[:, first : first + 1], left.shape)
    two = jnp.broadcast_to(columns[:, first + 1 : first + 2], left.shape)
    return jnp.where(left, one, two)


def left_half():
    return lax.broadcasted_iota(jnp.int32, (MAXLEN, LANES), 1) < HEAD_DIM


def delta_kernel(
    x_ref, b_ref, step_ref, cum_ref, delta_ref, kept_ref, *, heads
):
    step, cum = step_ref[0], cum_ref[0]
    last = cum[MAXLEN - 1 : MAXLEN, :]
    to_end = jnp.exp(last - cum) * step
    kept_ref[0] = jnp.broadcast_to(jnp.exp(last), kept_ref.shape[1:])
    left = left_half()
    in_proj = b_ref[...]
    per = delta_ref.shape[2]
    for first in range(0, heads, 2):
        lanes = slice(first * HEAD_DIM, (first + 2) * HEAD_DIM)
        scaled = x_ref[:, lanes].astype(jnp.float32) * spread(to_end, first, left)
        added = lax.dot_general(
            scaled.astype(jnp.bfloat16),
            in_proj,
            (((0,), (0,)), ((), ())),
            preferred_element_type=jnp.float32,
        )
        begin, count = first * HEAD_DIM // per, 2 * HEAD_DIM // per
        delta_ref[begin : begin + count, 0] = added.reshape(count, per, STATE)


def closing_kernel(start_ref, delta_ref, kept_ref, closing_ref, *, heads):
    per = start_ref.shape[2]
    count = HEAD_DIM // per
    for head in range(heads):
        rows = slice(head * count, (head + 1) * count)
        kept = kept_ref[0, :1, head : head + 1].reshape(1, 1, 1)
        closing = kept * start_ref[rows, 0].astype(jnp.float32) + delta_ref[rows, 0]
        closing_ref[rows, 0] = closing.astype(jnp.bfloat16)


def outputs_kernel(
    place_ref, sessions_ref, lengths_ref, x_ref, b_ref, c_ref, step_ref, cum_ref, start_ref,
    skip_ref, y_ref, *, heads, slot_count
):
    f32 = jnp.float32
    bf16 = jnp.bfloat16
    half = LANES
    width = heads * HEAD_DIM
    length = lengths_ref[sessions_ref[place_ref[0] * slot_count + pl.program_id(0)]]
    step, cum = step_ref[0], cum_ref[0]
    live = lax.broadcasted_iota(jnp.int32, (MAXLEN, LANES), 0) < length
    t_index = lax.broadcasted_iota(jnp.int32, (MAXLEN, MAXLEN), 0)
    u_index = lax.broadcasted_iota(jnp.int32, (MAXLEN, MAXLEN), 1)
    causal = t_index >= u_index
    drop_rows = (cum - jnp.log(step)).T
    grown = jnp.exp(cum)
    out_proj = c_ref[...]
    affinity = lax.dot_general(
        out_proj, b_ref[...], (((1,), (1,)), ((), ())), preferred_element_type=f32
    )
    affinity = jnp.where(causal, affinity, 0.0)
    top, low = affinity[:half, :half], affinity[half:, :]
    carried = lax.dot_general(
        out_proj,
        start_ref[...].reshape(width, STATE),
        (((1,), (1,)), ((), ())),
        preferred_element_type=f32,
    )
    left = left_half()
    for first in range(0, heads, 2):
        lanes = slice(first * HEAD_DIM, (first + 2) * HEAD_DIM)
        pair = x_ref[:, lanes]
        mixed = []
        for head in (first, first + 1):
            column = cum[:, head : head + 1]
            line = drop_rows[head : head + 1, :]
            w_top = top * jnp.exp(jnp.minimum(column[:half] - line[:, :half], 80.0))
            w_low = low * jnp.exp(jnp.minimum(column[half:] - line, 80.0))
            mixed.append(
                jnp.concatenate(
                    [
                        jnp.dot(w_top.astype(bf16), pair[:half], preferred_element_type=f32),
                        jnp.dot(w_low.astype(bf16), pair, preferred_element_type=f32),
                    ],
                    axis=0,
                )
            )
        out = (
            jnp.where(left, mixed[0], mixed[1])
            + spread(grown, first, left) * carried[:, lanes]
            + skip_ref[:, lanes] * pair.astype(f32)
        )
        y_ref[:, lanes] = jnp.where(live, out, 0.0).astype(bf16)


def session_call(kernel, scalars, slot_count, operands, outputs, flops, name):
    return pl.pallas_call(
        kernel,
        grid_spec=pltpu.PrefetchScalarGridSpec(
            num_scalar_prefetch=len(scalars),
            grid=(slot_count,),
            in_specs=[pl.BlockSpec(block, index) for _, block, index in operands],
            out_specs=[pl.BlockSpec(block, index) for _, block, index in outputs],
        ),
        out_shape=[shape for shape, _, _ in outputs],
        compiler_params=pltpu.CompilerParams(vmem_limit_bytes=VMEM_LIMIT),
        cost_estimate=pl.CostEstimate(
            flops=flops, bytes_accessed=8 * 1024 * 1024, transcendentals=0
        ),
        name=name,
    )(*scalars, *(array for array, _, _ in operands))


def per_device(
    x_in,
    dt_raw,
    b_in,
    c_in,
    a_log,
    dt_bias,
    d_skip,
    state_cache,
    group_sessions,
    owners,
    cache_slots,
    lengths,
):
    tensor_size = lax.axis_size("tensor")
    req_size = lax.axis_size("req")
    slot_count, heads = state_cache.shape[:2]
    per = heads * HEAD_DIM // req_size
    side = tensor_size // GROUPS
    rows = x_in.shape[0]
    width = heads * HEAD_DIM
    bf16 = jnp.bfloat16
    f32 = jnp.float32
    shape = jax.ShapeDtypeStruct
    req_index = lax.axis_index("req")
    tensor_index = lax.axis_index("tensor")
    place = jnp.stack(
        [req_index, tensor_index, tensor_index // side, tensor_index % side]
    ).astype(jnp.int32)
    sessions = group_sessions.reshape(-1)

    state_shape = (req_size, slot_count, per, STATE)
    table = cache_rows(sessions, owners, cache_slots, slot_count)
    pieces = state_cache.reshape(slot_count, req_size, per, STATE)
    held = exchange(pieces, req_size, 1).reshape(req_size * slot_count, per, STATE)
    held = reorder(held, table, False)

    extra = 2 * STATE + HEADS
    sent = local_call(
        pack_kernel,
        place,
        (x_in, dt_raw, b_in, c_in),
        [shape((rows, side * width + extra), bf16)] * GROUPS,
        "pack_tokens",
    )
    sent = local_call(
        turn_in_kernel,
        place,
        [send_along(sent, side, True)[shift] for shift in long_first(side)],
        [shape((GROUPS, rows, width + extra), bf16)] * side,
        "turn_in",
    )
    sent = send_along(sent, side, False)
    held, sent[side // 2] = lax.optimization_barrier((held, sent[side // 2]))
    start = exchange(held.reshape(state_shape), req_size)
    packed = local_call(
        gather_kernel,
        place,
        sent,
        shape((tensor_size, rows, width + extra), bf16),
        "gather_tokens",
    ).reshape(tensor_size * rows, width + extra)

    pad = ((0, 0), (0, LANES - slot_count * heads))
    a_row = jnp.pad(jnp.tile(a_log, slot_count)[None, :], pad)
    bias_row = jnp.pad(jnp.tile(dt_bias, slot_count)[None, :], pad)
    skip_row = jnp.repeat(d_skip, HEAD_DIM)[None, :]
    one_row = lambda j, *_: (0, 0)
    by_session = lambda j, *_: (j, 0)
    x_op = (packed, (MAXLEN, width), by_session)
    b_op = (packed, (MAXLEN, STATE), lambda j, *_: (j, width // STATE))
    c_op = (packed, (MAXLEN, STATE), lambda j, *_: (j, width // STATE + 1))
    skip_op = (skip_row, (1, width), one_row)
    scalars = (place, sessions, lengths)
    sizes = dict(heads=heads, slot_count=slot_count)
    piece_block = (req_size, 1, per, STATE)
    by_slot = lambda j, *_: (0, j, 0, 0)
    total_rows = tensor_size * rows

    kept_block = ((1, 8, LANES), lambda j, *_: (j, 0, 0))
    step, cum = pl.pallas_call(
        functools.partial(steps_kernel, heads=heads),
        grid_spec=pltpu.PrefetchScalarGridSpec(
            num_scalar_prefetch=len(scalars),
            grid=(1,),
            in_specs=[
                pl.BlockSpec((total_rows, HEADS), lambda j, *_: (0, width // HEADS + 2)),
                pl.BlockSpec((1, LANES), one_row),
                pl.BlockSpec((1, LANES), one_row),
            ],
            out_specs=[pl.BlockSpec((slot_count, MAXLEN, LANES), lambda j, *_: (0, 0, 0))] * 2,
        ),
        out_shape=[shape((slot_count, MAXLEN, LANES), f32)] * 2,
        compiler_params=pltpu.CompilerParams(vmem_limit_bytes=VMEM_LIMIT),
        name="steps",
    )(*scalars, packed, bias_row, a_row)
    step_block = ((1, MAXLEN, LANES), lambda j, *_: (j, 0, 0))
    step_op, cum_op = (step, *step_block), (cum, *step_block)

    delta, kept = session_call(
        functools.partial(delta_kernel, heads=heads),
        (),
        slot_count,
        [x_op, b_op, step_op, cum_op],
        [
            (pltpu.HBM(state_shape, f32), piece_block, by_slot),
            (shape((slot_count, 8, LANES), f32), *kept_block),
        ],
        4_000_000_000,
        "delta_states",
    )

    (closing,) = session_call(
        functools.partial(closing_kernel, heads=heads),
        (),
        slot_count,
        [(start, piece_block, by_slot), (delta, piece_block, by_slot), (kept, *kept_block)],
        [(pltpu.HBM(state_shape, bf16), piece_block, by_slot)],
        1_000_000_000,
        "closing_states",
    )
    closing, start = lax.optimization_barrier((closing, start))
    back = exchange(closing, req_size).reshape(req_size * slot_count, per, STATE)
    back = reorder(back, table, True)

    start_op = (start, piece_block, by_slot)
    (mixed,) = session_call(
        functools.partial(outputs_kernel, **sizes),
        scalars,
        slot_count,
        [x_op, b_op, c_op, step_op, cum_op, start_op, skip_op],
        [(shape((total_rows, width), bf16), (MAXLEN, width), by_session)],
        10_000_000_000,
        "session_outputs",
    )
    sent = local_call(
        split_kernel,
        place,
        (mixed.reshape(tensor_size, rows, width),),
        [shape((GROUPS, rows, width), bf16)] * side,
        "split_rows",
    )
    sent = local_call(
        turn_out_kernel,
        place,
        send_along(sent, side, False),
        [shape((rows, side * width), bf16)] * GROUPS,
        "turn_out",
    )
    back, *sent = lax.optimization_barrier((back, *sent))
    back = exchange(back.reshape(state_shape), req_size)
    new_cache = back.transpose(1, 0, 2, 3).reshape(state_cache.shape)
    y_out = local_call(
        columns_kernel,
        place,
        send_along(sent, side, True),
        shape(x_in.shape, bf16),
        "join_columns",
    )
    return y_out, new_cache


def solution(mesh):
    tokens = P(("req", "tensor"), None)
    states = P("req", "tensor", None, None)
    placed = (tokens,) * 4 + (P("tensor"),) * 3 + (states,) + (P(),) * 4
    return jax.shard_map(
        per_device,
        mesh=mesh,
        in_specs=placed,
        out_specs=(tokens, states),
        check_vma=False,
    )
```
